128 devices in a mesh: gz: 8 (over x, z_hi), gy: 4 (over z_lo, core), gx: 4 (over y).
Axes of the slice: x: 4, y: 4, z: 4 (z_hi: 2, z_lo: 2; z = z_hi * 2 + z_lo), core: 2. Of those that a mesh axis runs over, the one named last changes fastest.
Arguments:
- coeff_z: float32 [128, 128, 512], P('gz', 'gy', 'gx'), may hold values from 0.2 to 5
- coeff_y: float32 [128, 128, 512], P('gz', 'gy', 'gx'), may hold values from 0.2 to 5
- coeff_x: float32 [128, 128, 512], P('gz', 'gy', 'gx'), may hold values from 0.2 to 5
- reaction: float32 [128, 128, 512], P('gz', 'gy', 'gx'), may hold values from 0.1 to 2
Outputs:
- level_one: float32 [27, 64, 64, 256], P(None, 'gz', 'gy', 'gx')
- level_two: float32 [27, 32, 32, 128], P(None, 'gz', 'gy', 'gx')
- level_three: float32 [27, 16, 16, 64], P(None, 'gz')
The draws below stay inside these ranges and needn't reach their ends.
All inputs are finite; a program needn't handle non-finite values.
Results may differ from the reference program's by a relative error of at most 0.0003.
Values sent between devices are 32-bit elements; how exact they have to be, the bound alone decides.
A program may use at most 128 MiB of HBM per device.

```python
import math
from functools import partial
import jax
import jax.numpy as jnp
from jax import lax

NZ = 128
NY = 128
NX = 512


def steps_of(own_key, shape, split, low, largest):
    level, own = 1.0, jax.random.fold_in(own_key, 6)
    for position, shards_of in split:
        draws = jnp.exp(jax.random.uniform(jax.random.fold_in(own, position), (shards_of,), jnp.float32, low / len(split), largest / len(split)))
        level = level * jnp.repeat(draws, shape[position] // shards_of).reshape([-1 if axis == position else 1 for axis in range(len(shape))])
    return level


def setup_inputs(seed: int = 0) -> dict:
    keys = jax.random.split(jax.random.key(seed), 5)
    return {
        "coeff_z": jnp.clip(jnp.exp(math.log(5.0) - 3.218876 * jax.random.uniform(keys[0], (NZ, NY, NX), jnp.float32) ** steps_of(keys[0], (NZ, NY, NX), ((0, 8), (1, 4), (2, 4)), -0.2, 0.2)), 0.2, 5.0),
        "coeff_y": jnp.clip(jnp.exp(math.log(5.0) - 3.218876 * jax.random.uniform(keys[1], (NZ, NY, NX), jnp.float32) ** steps_of(keys[1], (NZ, NY, NX), ((0, 8), (1, 4), (2, 4)), -0.2, 0.2)), 0.2, 5.0),
        "coeff_x": jnp.clip(jnp.exp(math.log(5.0) - 3.218876 * jax.random.uniform(keys[2], (NZ, NY, NX), jnp.float32) ** steps_of(keys[2], (NZ, NY, NX), ((0, 8), (1, 4), (2, 4)), -0.2, 0.2)), 0.2, 5.0),
        "reaction": jnp.clip(jnp.exp(math.log(2.0) - 2.9957323 * jax.random.uniform(keys[3], (NZ, NY, NX), jnp.float32) ** steps_of(keys[3], (NZ, NY, NX), ((0, 8), (1, 4), (2, 4)), -0.2, 0.2)), 0.1, 2.0),
    }


def probe_lines(start, count, nfine, palette):
    places = start + jnp.arange(count, dtype=jnp.int32)
    ncoarse = nfine // 2

    def coarse_value(index):
        inside = (index >= 0) & (index < ncoarse)
        match = jnp.mod(index[None, :], 3) == palette[:, None]
        return jnp.where(match & inside[None, :], 1.0, 0.0).astype(jnp.float32)

    halves = jnp.floor_divide(places, 2)
    at_odd = coarse_value(halves)
    at_even = 0.5 * (coarse_value(halves - 1) + at_odd)
    value = jnp.where((jnp.mod(places, 2) == 1)[None, :], at_odd, at_even)
    return jnp.where(((places >= 0) & (places < nfine))[None, :], value, 0.0)


def select_lines(probe_sets, colours):
    match = colours[:, None] == jnp.arange(3, dtype=jnp.int32)[None, :]
    return jnp.sum(jnp.where(match[:, :, None], probe_sets[None, :, :], 0.0), axis=1)


def restrict_axis(field, axis):
    length = field.shape[axis] - 1
    lower = lax.slice_in_dim(field, 0, length, 2, axis)
    middle = lax.slice_in_dim(field, 1, length + 1, 2, axis)
    upper = lax.slice_in_dim(field, 2, length + 1, 2, axis)
    return 0.5 * lower + middle + 0.5 * upper


def window(block, lows, count):
    return lax.slice(block, (0, lows[0], lows[1], lows[2]),
                     (block.shape[0], lows[0] + count[0] + 1, lows[1] + count[1] + 1, lows[2] + count[2] + 1))


def fine_apply(padded, field, count):
    centre = window(field, (1, 1, 1), count)
    image = window(padded[3:4], (1, 1, 1), count) * centre
    image = image + window(padded[0:1], (1, 1, 1), count) * (centre - window(field, (2, 1, 1), count))
    image = image + window(padded[0:1], (0, 1, 1), count) * (centre - window(field, (0, 1, 1), count))
    image = image + window(padded[1:2], (1, 1, 1), count) * (centre - window(field, (1, 2, 1), count))
    image = image + window(padded[1:2], (1, 0, 1), count) * (centre - window(field, (1, 0, 1), count))
    image = image + window(padded[2:3], (1, 1, 1), count) * (centre - window(field, (1, 1, 2), count))
    image = image + window(padded[2:3], (1, 1, 0), count) * (centre - window(field, (1, 1, 0), count))
    return image


def stencil_apply(padded, field, count):
    image = jnp.zeros((field.shape[0], count[0] + 1, count[1] + 1, count[2] + 1), jnp.float32)
    for offset in range(27):
        shift_z = offset // 9 - 1
        shift_y = (offset // 3) % 3 - 1
        shift_x = offset % 3 - 1
        image = image + window(padded[offset:offset + 1], (1, 1, 1), count) * window(field, (1 + shift_z, 1 + shift_y, 1 + shift_x), count)
    return image


def galerkin(apply_fn, starts, count, totals, group):
    palette = jnp.arange(3, dtype=jnp.int32)
    probe_sets = [probe_lines(starts[axis] - 1, count[axis] + 3, totals[axis], palette) for axis in range(3)]
    limits = [(starts[axis] + jnp.arange(count[axis] + 1, dtype=jnp.int32)) < totals[axis] for axis in range(3)]
    inside = limits[0][:, None, None] & limits[1][None, :, None] & limits[2][None, None, :]

    def colour_block(number):
        colours = number * group + jnp.arange(group, dtype=jnp.int32)
        line_z = select_lines(probe_sets[0], colours // 9)
        line_y = select_lines(probe_sets[1], (colours // 3) % 3)
        line_x = select_lines(probe_sets[2], colours % 3)
        field = line_z[:, :, None, None] * line_y[:, None, :, None] * line_x[:, None, None, :]
        image = jnp.where(inside[None], apply_fn(field, count), 0.0)
        return 0.5 * restrict_axis(restrict_axis(restrict_axis(image, 1), 2), 3)

    blocks = lax.map(colour_block, jnp.arange(27 // group, dtype=jnp.int32))
    coarse_shape = blocks.shape[2:]
    products = blocks.reshape((3, 3, 3) + coarse_shape)
    choosers = []
    for axis in range(3):
        coarse = starts[axis] // 2 + jnp.arange(count[axis] // 2, dtype=jnp.int32)
        wanted = jnp.mod(coarse[None, :] + palette[:, None] - 1, 3)
        choosers.append(jnp.where(wanted[:, None, :] == palette[None, :, None], 1.0, 0.0).astype(jnp.float32))
    first_pass = jnp.sum(choosers[0][:, :, None, None, :, None, None] * products[None], axis=1)
    second_pass = jnp.sum(choosers[1][None, :, :, None, None, :, None] * first_pass[:, None], axis=2)
    third_pass = jnp.sum(choosers[2][None, None, :, :, None, None, :] * second_pass[:, :, None], axis=3)
    return third_pass.reshape((27,) + coarse_shape)


def reference(coeff_z, coeff_y, coeff_x, reaction):
    fine = jnp.stack([coeff_z, coeff_y, coeff_x, reaction])
    padding = ((0, 0), (1, 1), (1, 1), (1, 1))
    totals = (NZ, NY, NX)
    level_one = galerkin(partial(fine_apply, jnp.pad(fine, padding)), (0, 0, 0), totals, totals, 1)
    halves = (NZ // 2, NY // 2, NX // 2)
    level_two = galerkin(partial(stencil_apply, jnp.pad(level_one, padding)), (0, 0, 0), halves, halves, 1)
    quarters = (NZ // 4, NY // 4, NX // 4)
    level_three = galerkin(partial(stencil_apply, jnp.pad(level_two, padding)), (0, 0, 0), quarters, quarters, 1)
    return level_one, level_two, level_three
```

```python
from functools import partial

import jax
import jax.numpy as jnp
import ml_dtypes
import numpy as np
from jax import lax
from jax.experimental import pallas as pl
from jax.experimental.pallas import tpu as pltpu
from jax.sharding import PartitionSpec as P

MESH = pl.DeviceIdType.MESH
F32 = jnp.float32
BF16 = jnp.bfloat16


def forms(level, n):
    step = 1 << level
    i = np.arange(n)

    def hat(i, index):
        return np.maximum(0.0, 1.0 - np.abs(i - (step * index + step - 1)) / step)

    def slope(i, index):
        return hat(i, index) - hat(i + 1, index)

    def column(plus, index):
        other = index + plus
        return hat(i, index) * hat(i, other), slope(i, index) * slope(i, other)

    return column


def row_order(count):
    return (
        [(0, j) for j in range(count)]
        + [(1, j) for j in range(-1, count)]
        + [(0, -1), (0, count)]
    )


def weights_y(level, n, rows):
    column = forms(level, n)
    mass = np.zeros((rows, n))
    stiff = np.zeros((rows, n))
    for row, (plus, index) in enumerate(row_order(n >> level)):
        mass[row], stiff[row] = column(plus, index)
    first = np.concatenate([mass, mass, stiff, stiff], axis=1)
    second = np.concatenate([mass, mass], axis=1)
    return first.astype(ml_dtypes.bfloat16), second.astype(ml_dtypes.bfloat16)


def lanes_of(level, n):
    count = n >> level
    if level == 3:
        return [(0, j) for j in range(-1, count + 1)] + [(1, j) for j in range(-1, count)], 128
    rim = 2 * count
    lanes = [(0, j) for j in range(count)] + [(1, j) for j in range(count)]
    lanes += [None] * (2 * count)
    lanes[rim] = (0, -1)
    lanes[rim + count // 2] = (0, count)
    lanes[rim + count] = (1, -1)
    return lanes, 4 * count


def weights_x(level, n):
    column = forms(level, n)
    lanes, width = lanes_of(level, n)
    mass = np.zeros((n, width))
    stiff = np.zeros((n, width))
    for lane, entry in enumerate(lanes):
        if entry is not None:
            mass[:, lane], stiff[:, lane] = column(*entry)
    scale = 0.5**level
    both = np.concatenate([mass, mass, stiff, stiff], axis=0) * scale
    return both.astype(ml_dtypes.bfloat16)


def place_x(blocks, count):
    whole = blocks * count
    out = np.zeros((blocks, 2, 128, 3 * 128))
    for block in range(blocks):
        for layer in range(3):
            entries = lanes_of(3, count * 8)[0]
            for lane, (plus, index) in enumerate(entries):
                source = 40 * layer + lane
                target = block * count + index
                if 0 <= target < whole:
                    out[block, :, source, layer * 128 + plus * whole + target] = 1.0
                if plus == 0 and target == whole:
                    out[block, :, source, layer * 128 + whole - 1] = 63.0
                    out[block, :, source, layer * 128 + 2 * whole - 1] = 1.0
    return out.reshape(blocks * 256, 384).astype(ml_dtypes.bfloat16)


def place_y(blocks, count, rows, packed):
    whole = blocks * count
    out = np.zeros((rows, 2, blocks, packed))
    for block in range(blocks):
        for row, (plus, index) in enumerate(row_order(count)):
            target = block * count + index
            if 0 <= target < whole:
                out[target + plus * (whole + 1), :, block, row] = 1.0
            if plus == 0 and target == whole:
                out[whole - 1, :, block, row] = 63.0
                out[2 * whole, :, block, row] = 1.0
    return out.reshape(rows, 2 * blocks * packed).astype(ml_dtypes.bfloat16)


def split(value):
    high = value.astype(BF16)
    return high, (value - high.astype(F32)).astype(BF16)


def dot(left, right):
    return jnp.dot(left, right, preferred_element_type=F32)


def roll(value, shift):
    return pltpu.roll(value, shift % 128, 1)


def mass_layers(field):
    n = len(field)
    quarter = [0.25 * field[2 * j] for j in range(n // 2)] + [None]
    same = {-1: quarter[0]}
    plus = {-1: quarter[0]}
    for j in range(n // 2):
        total = field[2 * j + 1] + quarter[j]
        same[j] = total if quarter[j + 1] is None else total + quarter[j + 1]
        plus[j] = quarter[j + 1]
    same[n // 2] = None
    return same, plus


def stiff_layers(field):
    n = len(field)
    share = {-1: 0.25 * field[0], n // 2 - 1: 0.25 * field[n - 1]}
    for j in range(n // 2 - 1):
        share[j] = 0.25 * (field[2 * j + 1] + field[2 * j + 2])
    same = {-1: share[-1], n // 2: share[n // 2 - 1]}
    for j in range(n // 2):
        same[j] = share[j - 1] + share[j]
    return same, share


def plus_of(a, b):
    if a is None:
        return b
    return a if b is None else a + b


def coarser(same, plus, count):
    def scaled(value, factor):
        return None if value is None else factor * value

    new_same, new_plus = {}, {}
    half = count // 2
    for j in range(-1, half + 1):
        total = scaled(plus_of(same.get(2 * j), same.get(2 * j + 2)), 0.25)
        for term in (same.get(2 * j + 1), plus.get(2 * j), plus.get(2 * j + 1)):
            total = plus_of(total, term)
        new_same[j] = total
    for j in range(-1, half):
        total = scaled(plus_of(plus.get(2 * j + 1), plus.get(2 * j + 2)), 0.5)
        new_plus[j] = plus_of(total, scaled(same.get(2 * j + 2), 0.25))
    return new_same, new_plus


def main_kernel(
    r_ref, kz_ref, ky_ref, kx_ref,
    wy1a, wy1b, wy2a, wy2b, wy3a, wy3b, wx1, wx2, wx3,
    t1, x1, t2, x2, g3,
    ga1, gb1, ga2, gb2, ga3, gb3, c1, c2, c3,
    zu, zl, zr2, zr3, y1, y1r, y2, y2r, px1, px1r, px2, px2r, p3,
    send, recv, gsend, grecv,
):
    gz, gy, gx = lax.axis_index("gz"), lax.axis_index("gy"), lax.axis_index("gx")
    nz, ny, nx = lax.axis_size("gz"), lax.axis_size("gy"), lax.axis_size("gx")
    up_z, down_z = (lax.rem(gz + 1, nz), gy, gx), (lax.rem(gz + nz - 1, nz), gy, gx)
    up_y, down_y = (gz, lax.rem(gy + 1, ny), gx), (gz, lax.rem(gy + ny - 1, ny), gx)
    up_x, down_x = (gz, gy, lax.rem(gx + 1, nx)), (gz, gy, lax.rem(gx + nx - 1, nx))
    slab = ny * nx
    me = gy * nx + gx
    peers = []
    for d in range(1, slab):
        t = lax.rem(me + d, slab)
        peers.append((gz, lax.div(t, nx), lax.rem(t, nx)))

    barrier = pltpu.get_barrier_semaphore()
    for device in peers + [up_z, down_z]:
        pl.semaphore_signal(barrier, inc=1, device_id=device, device_id_type=MESH)
    pl.semaphore_wait(barrier, slab + 1)

    started = []

    def copy(src, dst, device):
        k = len(started)
        c = pltpu.make_async_remote_copy(
            src_ref=src, dst_ref=dst, send_sem=send.at[k], recv_sem=recv.at[k],
            device_id=device, device_id_type=MESH,
        )
        c.start()
        started.append(c)
        return c

    raw = [
        copy(f.at[0], zu.at[j], down_z) for j, f in enumerate((r_ref, kz_ref, ky_ref, kx_ref))
    ]
    raw.append(copy(kz_ref.at[15], zl, up_z))

    def layers(ref):
        return [ref[j] for j in range(16)]

    kz_layers = layers(kz_ref)
    same1, plus1 = mass_layers(layers(r_ref))
    ssame, share = stiff_layers(kz_layers)
    for j in range(-1, 9):
        same1[j] = plus_of(same1[j], ssame[j])
    for j in range(-1, 8):
        plus1[j] = -share[j] if plus1[j] is None else plus1[j] - share[j]
    level1 = [(same1, plus1), mass_layers(layers(ky_ref)), mass_layers(layers(kx_ref))]
    level2 = [coarser(*f, 8) for f in level1]
    level3 = [coarser(*f, 4) for f in level2]

    zero = jnp.zeros((32, 128), F32)

    def put(ga, gb, j, fields):
        lanes = pl.ds(128 * j, 128)
        for base, (ref, value) in enumerate(zip((ga, ga, gb), fields)):
            high, low = split(zero if value is None else value)
            start = 64 * base if base < 2 else 0
            ref[start:start + 32, lanes] = high
            ref[start + 32:start + 64, lanes] = low

    def reduce_yx(ga, gb, wya, wyb, wx, count, rows):
        first = dot(wya[...], ga[...])
        second = dot(wyb[...], gb[...])
        left = []
        for value in (first, second):
            stacked = jnp.concatenate(
                [value[:, 128 * j:128 * j + 128] for j in range(count)], axis=0
            )
            left += split(stacked)
        out = dot(jnp.concatenate(left, axis=1), wx[...])
        return out.reshape(count, rows, out.shape[1])

    for j, (plus, index) in enumerate(row_order(2)):
        put(ga3, gb3, j, [f[plus][index] for f in level3])
    c3[...] = reduce_yx(ga3, gb3, wy3a, wy3b, wx3, 7, 16)
    for j, (plus, index) in enumerate(row_order(4)):
        put(ga2, gb2, j, [f[plus][index] for f in level2])
    c2[...] = reduce_yx(ga2, gb2, wy2a, wy2b, wx2, 11, 32)

    round_z = [
        copy(c2.at[9, 0:24], zr2.at[0], down_z),
        copy(c2.at[4, 0:24], zr2.at[1], down_z),
        copy(c2.at[10, 0:24], zr2.at[2], up_z),
        copy(c3.at[5], zr3.at[0], down_z),
        copy(c3.at[2], zr3.at[1], down_z),
        copy(c3.at[6], zr3.at[2], up_z),
    ]

    top_z, low_z = gz == nz - 1, gz == 0
    for c in raw:
        c.wait_recv()
    last = share[7]
    up_r, up_kz = 0.25 * zu[0], 0.25 * zu[1]
    up_ky, up_kx = 0.25 * zu[2], 0.25 * zu[3]
    come = jnp.where(low_z, 0.0, 0.25 * zl[...])
    add_same = [jnp.where(top_z, 3.0 * last, up_r + up_kz)]
    add_plus = [jnp.where(top_z, last, up_r - up_kz)]
    for f in (up_ky, up_kx):
        add_same.append(jnp.where(top_z, 0.0, f))
        add_plus.append(add_same[-1])
    for f in range(3):
        same, plus = level1[f]
        same[7] = plus_of(same[7], add_same[f])
        plus[7] = plus_of(plus[7], add_plus[f])
        if f == 0:
            same[0] = same[0] + come
            plus[-1] = plus[-1] - come
        plus[-1] = jnp.where(low_z, 0.0, plus[-1])

    for j, (plus, index) in enumerate(row_order(8)[:17]):
        put(ga1, gb1, j, [f[plus][index] for f in level1])
    c1[...] = reduce_yx(ga1, gb1, wy1a, wy1b, wx1, 17, 48)

    for c in round_z:
        c.wait_recv()

    def fix_z(c, came, n, rows, factor):
        same_up, plus_up, share_low = came[0], came[1], came[2]
        rim = c[2 * n + 2, 0:rows]
        low = jnp.where(low_z, 0.0, share_low)
        out = {
            n - 1: c[n - 1, 0:rows] + jnp.where(top_z, factor * rim, same_up),
            2 * n: c[2 * n, 0:rows] + jnp.where(top_z, rim, plus_up),
            n: jnp.where(low_z, 0.0, c[n, 0:rows] - low),
        }
        for k, value in out.items():
            pass
        return out, low

    for c in round_z:
        c.wait_send()
    out2, low2 = fix_z(c2, zr2, 4, 24, 15.0)
    out3, low3 = fix_z(c3, zr3, 2, 16, 63.0)
    for k, value in out2.items():
        c2[k, 0:24] = value
    c2[0, 0:24] = c2[0, 0:24] + low2
    for k, value in out3.items():
        c3[k] = value
    c3[0] = c3[0] + low3

    for h in range(2):
        total = c3[3 * h]
        for j in range(1, 3):
            if 3 * h + j < 5:
                total = total + roll(c3[3 * h + j], 40 * j)
        p3[h] = total
    g3[pl.ds(me, 1)] = p3[...][None]
    gather = []
    for d, device in enumerate(peers):
        c = pltpu.make_async_remote_copy(
            src_ref=p3, dst_ref=g3.at[me], send_sem=gsend.at[d], recv_sem=grecv.at[d],
            device_id=device, device_id_type=MESH,
        )
        c.start()
        gather.append(c)

    sets = ((c1, y1, y1r, 17, 16, 3.0), (c2, y2, y2r, 9, 8, 15.0))
    for c, y, _, count, n, _ in sets:
        for j in range(count):
            for k, row in enumerate((2 * n + 1, n, 2 * n + 2)):
                y[k, j:j + 1] = c[j, row:row + 1]
    round_y = []
    for _, y, yr, _, _, _ in sets:
        round_y.append(copy(y.at[0:2], yr.at[0:2], down_y))
        round_y.append(copy(y.at[2], yr.at[2], up_y))
    top_y, low_y = gy == ny - 1, gy == 0
    for c in round_y:
        c.wait_recv()
    for c, y, yr, count, n, factor in sets:
        rim = y[2]
        same_up = jnp.where(top_y, factor * rim, yr[0])
        plus_up = jnp.where(top_y, rim, yr[1])
        low = jnp.where(low_y, 0.0, yr[2])
        first = jnp.where(low_y, 0.0, y[1] - low)
        for j in range(count):
            c[j, n - 1:n] = c[j, n - 1:n] + same_up[j:j + 1]
            c[j, 2 * n:2 * n + 1] = c[j, 2 * n:2 * n + 1] + plus_up[j:j + 1]
            c[j, 0:1] = c[j, 0:1] + low[j:j + 1]
            c[j, n:n + 1] = first[j:j + 1]

    top_x, low_x = gx == nx - 1, gx == 0
    sets = ((c1, px1, px1r, t1, x1, 17, 40, 64, 3.0), (c2, px2, px2r, t2, x2, 9, 24, 32, 15.0))
    round_x = []
    for c, px, pxr, _, _, count, rows, n, _ in sets:
        lane = lax.broadcasted_iota(jnp.int32, (rows, 128), 1)
        total = None
        for j in range(count):
            if n == 64:
                part = roll(c[j, 0:rows, 128:256], j)
            else:
                part = roll(jnp.where(lane >= 64, c[j, 0:rows], 0.0), 64 + j)
            total = part if total is None else total + part
        px[...] = total
        round_x.append(copy(px, pxr.at[0], down_x))
        round_x.append(copy(px, pxr.at[1], up_x))
    for c in round_x:
        c.wait_recv()
    for c, px, pxr, t, x, count, rows, n, factor in sets:
        lane = lax.broadcasted_iota(jnp.int32, (rows, 128), 1)
        own = px[...]
        edge = jnp.where(lane < n // 2, factor * roll(own, -(n // 2)), roll(own, n // 2))
        above = jnp.where(top_x, edge, pxr[0])
        below = jnp.where(low_x, 0.0, pxr[1])
        x[...] = jnp.where(low_x, 0.0, own - roll(below, n // 2))
        at_end = (lane == n - 1) | (lane == 2 * n - 1)
        for j in range(count):
            value = c[j, 0:rows, 0:128]
            value = value + jnp.where(at_end, roll(above, n - 1 - j), 0.0)
            t[j] = value + jnp.where(lane == 0, roll(below, -(n // 2) - j), 0.0)

    for c in gather:
        c.wait()
    for c in raw + round_y + round_x:
        c.wait_send()


def expand_kernel(t1, x1, t2, x2, g3, qx, qy, o1, o2, o3, q3, s3):
    blocks = [[g3[4 * by + bx].reshape(32, 128) for by in range(4)] for bx in range(4)]
    left = []
    for bx in range(4):
        left += split(jnp.concatenate(blocks[bx], axis=0))
    q3[...] = dot(jnp.concatenate(left, axis=1), qx[...])
    for h in range(2):
        rows = jnp.concatenate(
            [q3[32 * by + 16 * h:32 * by + 16 * h + 16, :] for by in range(4)], axis=0
        )
        placed = dot(qy[...], jnp.concatenate(split(rows), axis=0))
        for j in range(3):
            if 3 * h + j < 5:
                s3[3 * h + j] = placed[0:40, 128 * j:128 * j + 128]

    def expand(t, x, o, nz, ny, n):
        def planes(k):
            value = t[k]
            lane = lax.broadcasted_iota(jnp.int32, value.shape, 1)
            first = 0.0 if x is None else roll(x[...], -(n + k))
            low = jnp.where(lane == 0, first, roll(value, 1 - n))
            return (low, value, roll(value, -n))

        for k in range(2 * nz + 1):
            for c, plane in enumerate(planes(k)):
                plane = plane[:, 0:n]
                if k < nz:
                    targets = [(1, k)]
                else:
                    targets = [(0, k - nz)] if k - nz < nz else []
                    targets += [(2, k - nz - 1)] if k > nz else []
                for a, layer in targets:
                    o[9 * a + c, layer] = plane[ny:2 * ny]
                    o[9 * a + 3 + c, layer] = plane[0:ny]
                    o[9 * a + 6 + c, layer] = plane[ny + 1:2 * ny + 1]

    expand(s3, None, o3, 2, 16, 64)
    expand(t2, x2, o2, 4, 8, 32)
    expand(t1, x1, o1, 8, 16, 64)


def shards(coeff_z, coeff_y, coeff_x, reaction):
    consts = []
    for level, rows in ((1, 48), (2, 32), (3, 16)):
        consts += weights_y(level, 32, rows)
    for level in (1, 2, 3):
        consts.append(weights_x(level, 128))
    vmem = pl.BlockSpec(memory_space=pltpu.VMEM)
    shape = jax.ShapeDtypeStruct
    v = pltpu.VMEM
    t1, x1, t2, x2, g3 = pl.pallas_call(
        main_kernel,
        out_shape=(
            shape((17, 40, 128), F32), shape((40, 128), F32),
            shape((9, 24, 128), F32), shape((24, 128), F32),
            shape((16, 2, 16, 128), F32),
        ),
        in_specs=[vmem] * 13,
        out_specs=(vmem,) * 5,
        scratch_shapes=[
            v((128, 17 * 128), BF16), v((64, 17 * 128), BF16),
            v((128, 11 * 128), BF16), v((64, 11 * 128), BF16),
            v((128, 7 * 128), BF16), v((64, 7 * 128), BF16),
            v((17, 48, 256), F32), v((11, 32, 128), F32), v((7, 16, 128), F32),
            v((4, 32, 128), F32), v((32, 128), F32), v((3, 24, 128), F32), v((3, 16, 128), F32),
            v((3, 24, 256), F32), v((3, 24, 256), F32), v((3, 16, 128), F32), v((3, 16, 128), F32),
            v((40, 128), F32), v((2, 40, 128), F32), v((24, 128), F32), v((2, 24, 128), F32),
            v((2, 16, 128), F32),
            pltpu.SemaphoreType.DMA((19,)), pltpu.SemaphoreType.DMA((19,)),
            pltpu.SemaphoreType.DMA((15,)), pltpu.SemaphoreType.DMA((15,)),
        ],
        compiler_params=pltpu.CompilerParams(
            collective_id=0, has_side_effects=True, vmem_limit_bytes=32 << 20
        ),
    )(reaction, coeff_z, coeff_y, coeff_x, *map(jnp.asarray, consts))
    return pl.pallas_call(
        expand_kernel,
        out_shape=(
            shape((27, 8, 16, 64), F32), shape((27, 4, 8, 32), F32), shape((27, 2, 16, 64), F32),
        ),
        in_specs=[vmem] * 7,
        out_specs=(vmem,) * 3,
        scratch_shapes=[v((128, 384), F32), v((5, 40, 128), F32)],
        compiler_params=pltpu.CompilerParams(vmem_limit_bytes=32 << 20),
    )(t1, x1, t2, x2, g3, jnp.asarray(place_x(4, 16)), jnp.asarray(place_y(4, 4, 48, 16)))


def solution(mesh):
    in_specs = (P("gz", "gy", "gx"),) * 4
    out_specs = (P(None, "gz", "gy", "gx"), P(None, "gz", "gy", "gx"), P(None, "gz", None, None))
    return jax.shard_map(shards, mesh=mesh, in_specs=in_specs, out_specs=out_specs, check_vma=False)
```

```python
from functools import partial

import jax
import jax.numpy as jnp
import ml_dtypes
import numpy as np
from jax import lax
from jax.experimental import pallas as pl
from jax.experimental.pallas import tpu as pltpu
from jax.sharding import PartitionSpec as P

MESH = pl.DeviceIdType.MESH
F32 = jnp.float32
BF16 = jnp.bfloat16


def forms(level, n):
    step = 1 << level
    i = np.arange(n)

    def hat(i, index):
        return np.maximum(0.0, 1.0 - np.abs(i - (step * index + step - 1)) / step)

    def slope(i, index):
        return hat(i, index) - hat(i + 1, index)

    def column(plus, index):
        other = index + plus
        return hat(i, index) * hat(i, other), slope(i, index) * slope(i, other)

    return column


def row_order(count):
    return (
        [(0, j) for j in range(count)]
        + [(1, j) for j in range(-1, count)]
        + [(0, -1), (0, count)]
    )


def y_rows(level, count):
    order = row_order(count)
    if level == 3:
        return dict(zip(order, range(len(order))))
    place = {(0, j): j for j in range(count)}
    place.update({(1, j): count + 8 + j for j in range(count)})
    place.update({(0, -1): count + 5, (0, count): count + 6, (1, -1): count + 7})
    return place


def weights_y(level, n, rows):
    column = forms(level, n)
    mass = np.zeros((rows, n))
    stiff = np.zeros((rows, n))
    for (plus, index), row in y_rows(level, n >> level).items():
        mass[row], stiff[row] = column(plus, index)
    first = np.concatenate([mass, mass, stiff, stiff], axis=1)
    second = np.concatenate([mass, mass], axis=1)
    return first, second


def lanes_of(level, n):
    count = n >> level
    if level == 3:
        return [(0, j) for j in range(-1, count + 1)] + [(1, j) for j in range(-1, count)], 128
    rim = 2 * count
    lanes = [(0, j) for j in range(count)] + [(1, j) for j in range(count)]
    lanes += [None] * (2 * count)
    lanes[rim] = (0, -1)
    lanes[rim + count // 2] = (0, count)
    lanes[rim + count] = (1, -1)
    return lanes, 4 * count


def weights_x(level, n):
    column = forms(level, n)
    lanes, width = lanes_of(level, n)
    mass = np.zeros((n, width))
    stiff = np.zeros((n, width))
    for lane, entry in enumerate(lanes):
        if entry is not None:
            mass[:, lane], stiff[:, lane] = column(*entry)
    scale = 0.5**level
    both = np.concatenate([mass, mass, stiff, stiff], axis=0) * scale
    return both


def place_x(blocks, count):
    whole = blocks * count
    out = np.zeros((blocks, 2, 128, 3 * 128))
    for block in range(blocks):
        for layer in range(3):
            entries = lanes_of(3, count * 8)[0]
            for lane, (plus, index) in enumerate(entries):
                source = 40 * layer + lane
                target = block * count + index
                if 0 <= target < whole:
                    out[block, :, source, layer * 128 + plus * whole + target] = 1.0
                if plus == 0 and target == whole:
                    out[block, :, source, layer * 128 + whole - 1] = 63.0
                    out[block, :, source, layer * 128 + 2 * whole - 1] = 1.0
    return out.reshape(blocks * 256, 384).astype(ml_dtypes.bfloat16)


def place_y(blocks, count, rows, packed):
    whole = blocks * count
    out = np.zeros((rows, 2, blocks, packed))
    for block in range(blocks):
        for row, (plus, index) in enumerate(row_order(count)):
            target = block * count + index
            if 0 <= target < whole:
                out[target + plus * (whole + 8), :, block, row] = 1.0
            if plus == 0 and target == whole:
                out[whole - 1, :, block, row] = 63.0
                out[2 * whole + 7, :, block, row] = 1.0
    return out.reshape(rows, 2 * blocks * packed).astype(ml_dtypes.bfloat16)


def split(value):
    high = value.astype(BF16)
    return high, (value - high.astype(F32)).astype(BF16)


def dot(left, right):
    return jnp.dot(left, right, preferred_element_type=F32)


def roll(value, shift):
    return pltpu.roll(value, shift % 128, 1)


def mass_layers(field):
    n = len(field)
    quarter = [0.25 * field[2 * j] for j in range(n // 2)] + [None]
    same = {-1: quarter[0]}
    plus = {-1: quarter[0]}
    for j in range(n // 2):
        total = field[2 * j + 1] + quarter[j]
        same[j] = total if quarter[j + 1] is None else total + quarter[j + 1]
        plus[j] = quarter[j + 1]
    same[n // 2] = None
    return same, plus


def stiff_layers(field):
    n = len(field)
    share = {-1: 0.25 * field[0], n // 2 - 1: 0.25 * field[n - 1]}
    for j in range(n // 2 - 1):
        share[j] = 0.25 * (field[2 * j + 1] + field[2 * j + 2])
    same = {-1: share[-1], n // 2: share[n // 2 - 1]}
    for j in range(n // 2):
        same[j] = share[j - 1] + share[j]
    return same, share


def plus_of(a, b):
    if a is None:
        return b
    return a if b is None else a + b


def coarser(same, plus, count):
    def scaled(value, factor):
        return None if value is None else factor * value

    new_same, new_plus = {}, {}
    half = count // 2
    for j in range(-1, half + 1):
        total = scaled(plus_of(same.get(2 * j), same.get(2 * j + 2)), 0.25)
        for term in (same.get(2 * j + 1), plus.get(2 * j), plus.get(2 * j + 1)):
            total = plus_of(total, term)
        new_same[j] = total
    for j in range(-1, half):
        total = scaled(plus_of(plus.get(2 * j + 1), plus.get(2 * j + 2)), 0.5)
        new_plus[j] = plus_of(total, scaled(same.get(2 * j + 2), 0.25))
    return new_same, new_plus


def all_weights():
    out = np.zeros((576, 512))
    for level, start, width in ((1, 0, 256), (2, 256, 128), (3, 384, 128)):
        out[:512, start:start + width] = weights_x(level, 128)
    for level, row, rows, lane in ((1, 512, 48, 0), (2, 512, 32, 256), (3, 560, 16, 0)):
        first, second = weights_y(level, 32, rows)
        out[row:row + rows, lane:lane + 128] = first
        out[row:row + rows, lane + 128:lane + 192] = second
    return out.astype(ml_dtypes.bfloat16)


def main_kernel(
    r_hbm, kz_hbm, ky_hbm, kx_hbm, w_hbm,
    t1, x1, t2, x2, g3,
    f4, w, zs, zu, zl, rims, rimr,
    ga1, gb1, ga2, gb2, ga3, gb3, c2, c3,
    yb, yr, px, pxr, pxf, dr, p3,
    lsem, send, recv, gsend, grecv,
):
    gz, gy, gx = lax.axis_index("gz"), lax.axis_index("gy"), lax.axis_index("gx")
    nz, ny, nx = lax.axis_size("gz"), lax.axis_size("gy"), lax.axis_size("gx")
    zp, zm = lax.rem(gz + 1, nz), lax.rem(gz + nz - 1, nz)
    yp, ym = lax.rem(gy + 1, ny), lax.rem(gy + ny - 1, ny)
    xp, xm = lax.rem(gx + 1, nx), lax.rem(gx + nx - 1, nx)
    slab = ny * nx
    me = gy * nx + gx
    peers = []
    for d in range(1, slab):
        t = lax.rem(me + d, slab)
        peers.append((gz, lax.div(t, nx), lax.rem(t, nx)))

    barrier = pltpu.get_barrier_semaphore()
    for device in [(zp, gy, gx), (zm, gy, gx)] + peers:
        pl.semaphore_signal(barrier, inc=1, device_id=device, device_id_type=MESH)

    fields = (r_hbm, kz_hbm, ky_hbm, kx_hbm)
    first = [pltpu.make_async_copy(f.at[0], zs.at[j], lsem.at[j]) for j, f in enumerate(fields)]
    first.append(pltpu.make_async_copy(kz_hbm.at[15], zs.at[4], lsem.at[4]))
    bulk = [pltpu.make_async_copy(f, f4.at[j], lsem.at[5 + j]) for j, f in enumerate(fields)]
    bulk.append(pltpu.make_async_copy(w_hbm, w, lsem.at[9]))
    for c in first + bulk:
        c.start()

    started = []

    def copy(src, dst, device):
        k = len(started)
        c = pltpu.make_async_remote_copy(
            src_ref=src, dst_ref=dst, send_sem=send.at[k], recv_sem=recv.at[k],
            device_id=device, device_id_type=MESH,
        )
        c.start()
        started.append(c)
        return c

    for c in first:
        c.wait()
    pl.semaphore_wait(barrier, slab + 1)
    raw = [copy(zs.at[0:4], zu, (zm, gy, gx)), copy(zs.at[4], zl, (zp, gy, gx))]
    for c in bulk:
        c.wait()

    def layers(j):
        return [f4[j, k] for k in range(16)]

    same1, plus1 = mass_layers(layers(0))
    ssame, share = stiff_layers(layers(1))
    for j in range(-1, 9):
        same1[j] = plus_of(same1[j], ssame[j])
    for j in range(-1, 8):
        plus1[j] = -share[j] if plus1[j] is None else plus1[j] - share[j]
    level1 = [(same1, plus1), mass_layers(layers(2)), mass_layers(layers(3))]
    level2 = [coarser(*f, 8) for f in level1]
    level3 = [coarser(*f, 4) for f in level2]

    zero = jnp.zeros((32, 128), F32)

    def put(ga, gb, j, values):
        lanes = pl.ds(128 * j, 128)
        for base, (ref, value) in enumerate(zip((ga, ga, gb), values)):
            high, low = split(zero if value is None else value)
            start = 64 * base if base < 2 else 0
            ref[start:start + 32, lanes] = high
            ref[start + 32:start + 64, lanes] = low

    def reduce_yx(ga, gb, wya, wyb, wx, start, count, rows):
        lanes = pl.ds(128 * start, 128 * count)
        left = []
        for value in (dot(wya, ga[:, lanes]), dot(wyb, gb[:, lanes])):
            stacked = jnp.concatenate(
                [value[:, 128 * j:128 * j + 128] for j in range(count)], axis=0
            )
            left += split(stacked)
        out = dot(jnp.concatenate(left, axis=1), wx)
        return [out[rows * j:rows * j + rows] for j in range(count)]

    for j, (plus, index) in enumerate(row_order(2)):
        put(ga3, gb3, j, [f[plus][index] for f in level3])
    for j, (plus, index) in enumerate(row_order(4)):
        put(ga2, gb2, j, [f[plus][index] for f in level2])
    out3 = reduce_yx(
        ga3, gb3, w[560:576, 0:128], w[560:576, 128:192], w[0:512, 384:512], 0, 7, 16
    )
    out2 = reduce_yx(
        ga2, gb2, w[512:544, 256:384], w[512:544, 384:448], w[0:512, 256:384], 0, 11, 32
    )
    for k, (j3, j2) in enumerate(((5, 9), (2, 4), (6, 10))):
        rims[k, 0:24] = out2[j2][0:24]
        rims[k, 24:40] = out3[j3]
    for j in range(9):
        c2[j] = out2[j][0:24]
    for j in range(5):
        c3[j] = out3[j]
    round_z = [
        copy(rims.at[0:2], rimr.at[0:2], (zm, gy, gx)),
        copy(rims.at[2], rimr.at[2], (zp, gy, gx)),
    ]

    order1 = row_order(8)
    inner = list(range(1, 7)) + list(range(9, 16))
    outer = [0, 7, 8, 16]
    x_total = [None, None]

    def level_one(start, places):
        for j, k in enumerate(places):
            plus, index = order1[k]
            put(ga1, gb1, start + j, [f[plus][index] for f in level1])
        out = reduce_yx(
            ga1, gb1, w[512:560, 0:128], w[512:560, 128:192], w[0:512, 0:256],
            start, len(places), 48,
        )
        for k, value in zip(places, out):
            t1[k] = value[0:40, 0:128]
            x_total[0] = plus_of(x_total[0], roll(value[0:40, 128:256], k))
            for slot, row in ((0, 21), (1, 23), (3, 22)):
                yb[slot, k:k + 1] = value[row:row + 1, 0:128]

    level_one(0, inner)

    top_z, low_z = gz == nz - 1, gz == 0
    for c in raw:
        c.wait_recv()
    last = share[7]
    up_r, up_kz = 0.25 * zu[0], 0.25 * zu[1]
    up_ky, up_kx = 0.25 * zu[2], 0.25 * zu[3]
    come = jnp.where(low_z, 0.0, 0.25 * zl[...])
    add_same = [jnp.where(top_z, 3.0 * last, up_r + up_kz)]
    add_plus = [jnp.where(top_z, last, up_r - up_kz)]
    for f in (up_ky, up_kx):
        add_same.append(jnp.where(top_z, 0.0, f))
        add_plus.append(add_same[-1])
    for f in range(3):
        same, plus = level1[f]
        same[7] = plus_of(same[7], add_same[f])
        plus[7] = plus_of(plus[7], add_plus[f])
        if f == 0:
            same[0] = same[0] + come
            plus[-1] = plus[-1] - come
        plus[-1] = jnp.where(low_z, 0.0, plus[-1])
    level_one(13, outer)

    for c in round_z:
        c.wait_recv()
    rim = rims[2]
    factor = jnp.where(lax.broadcasted_iota(jnp.int32, (40, 128), 0) < 24, 15.0, 63.0)
    same_up = jnp.where(top_z, factor * rim, rimr[0])
    plus_up = jnp.where(top_z, rim, rimr[1])
    low = jnp.where(low_z, 0.0, rimr[2])
    fix2 = {0: low, 3: same_up, 4: -low, 8: plus_up}
    fix3 = {0: low, 1: same_up, 2: -low, 4: plus_up}
    lane2 = lax.broadcasted_iota(jnp.int32, (24, 128), 1)
    for j in range(9):
        value = c2[j] if j not in fix2 else c2[j] + fix2[j][0:24]
        if j == 4:
            value = jnp.where(low_z, 0.0, value)
        t2[j] = value
        x_total[1] = plus_of(x_total[1], roll(jnp.where(lane2 >= 64, value, 0.0), 64 + j))
        for slot, row in ((0, 13), (1, 15), (3, 14)):
            yb[slot, 24 + j:25 + j] = value[row:row + 1]
    packed = [None, None]
    for j in range(5):
        value = c3[j] if j not in fix3 else c3[j] + fix3[j][24:40]
        if j == 2:
            value = jnp.where(low_z, 0.0, value)
        packed[j // 3] = plus_of(packed[j // 3], roll(value, 40 * (j % 3)) if j % 3 else value)

    px[0:40] = x_total[0]
    px[40:64] = x_total[1]
    yb[2, 0:8] = x_total[0][16:24]
    yb[2, 8:16] = x_total[1][8:16]
    p3[0] = packed[0]
    p3[1] = packed[1]
    round_yx = [
        copy(px, pxr.at[0], (gz, gy, xm)),
        copy(px, pxr.at[1], (gz, gy, xp)),
        copy(yb.at[0:3], yr.at[0, 0:3], (gz, ym, gx)),
        copy(yb.at[2:4], yr.at[1, 2:4], (gz, yp, gx)),
        copy(yb.at[2, 0:16], dr.at[0], (gz, ym, xm)),
        copy(yb.at[2, 0:16], dr.at[1], (gz, ym, xp)),
        copy(yb.at[2, 0:16], dr.at[2], (gz, yp, xm)),
        copy(yb.at[2, 0:16], dr.at[3], (gz, yp, xp)),
    ]
    gather = []
    for d, device in enumerate(peers):
        c = pltpu.make_async_remote_copy(
            src_ref=p3, dst_ref=g3.at[me], send_sem=gsend.at[d], recv_sem=grecv.at[d],
            device_id=device, device_id_type=MESH,
        )
        c.start()
        gather.append(c)
    g3[pl.ds(me, 1)] = p3[...][None]

    top_y, low_y = gy == ny - 1, gy == 0
    top_x, low_x = gx == nx - 1, gx == 0
    for c in round_yx:
        c.wait_recv()

    for t, first, count, n, factor in ((t1, 0, 17, 16, 3.0), (t2, 24, 9, 8, 15.0)):
        span = slice(first, first + (24 if n == 16 else 16))
        rim = yb[3, span]
        same_up = jnp.where(top_y, factor * rim, yr[0, 0, span])
        plus_up = jnp.where(top_y, rim, yr[0, 1, span])
        low = jnp.where(low_y, 0.0, yr[1, 3, span])
        bottom = jnp.where(low_y, 0.0, yb[1, span] - low)
        for j in range(count):
            t[j, n - 1:n] = t[j, n - 1:n] + same_up[j:j + 1]
            t[j, 2 * n + 7:2 * n + 8] = t[j, 2 * n + 7:2 * n + 8] + plus_up[j:j + 1]
            t[j, 0:1] = t[j, 0:1] + low[j:j + 1]
            t[j, n + 7:n + 8] = bottom[j:j + 1]

    sources = (
        (px, yr.at[0, 2], yr.at[1, 2]),
        (pxr.at[0], dr.at[0], dr.at[2]),
        (pxr.at[1], dr.at[1], dr.at[3]),
    )
    for k, (source, upper, lower) in enumerate(sources):
        pxf[k] = source[...]
        for base, group, n, factor in ((0, 0, 16, 3.0), (40, 8, 8, 15.0)):
            rim = source[base + n + 6:base + n + 7]
            same_up = jnp.where(top_y, factor * rim, upper[group + 5:group + 6])
            plus_up = jnp.where(top_y, rim, upper[group + 7:group + 8])
            low = jnp.where(low_y, 0.0, lower[group + 6:group + 7])
            for row, value in ((n - 1, same_up), (2 * n + 7, plus_up), (0, low)):
                at = slice(base + row, base + row + 1)
                pxf[k, at] = pxf[k, at] + value
            at = slice(base + n + 7, base + n + 8)
            pxf[k, at] = jnp.where(low_y, 0.0, pxf[k, at] - low)

    sets = ((t1, x1, 17, 0, 40, 64, 3.0), (t2, x2, 9, 40, 24, 32, 15.0))
    for t, x, count, base, rows, n, factor in sets:
        lane = lax.broadcasted_iota(jnp.int32, (rows, 128), 1)
        own = pxf[0, base:base + rows]
        edge = jnp.where(lane < n // 2, factor * roll(own, -(n // 2)), roll(own, n // 2))
        above = jnp.where(top_x, edge, pxf[1, base:base + rows])
        below = jnp.where(low_x, 0.0, pxf[2, base:base + rows])
        x[...] = jnp.where(low_x, 0.0, own - roll(below, n // 2))
        at_end = (lane == n - 1) | (lane == 2 * n - 1)
        for j in range(count):
            value = t[j] + jnp.where(at_end, roll(above, n - 1 - j), 0.0)
            t[j] = value + jnp.where(lane == 0, roll(below, -(n // 2) - j), 0.0)

    for c in gather:
        c.wait()
    for c in started:
        c.wait_send()


def expand_kernel(
    t1, x1, t2, x2, g3, qx_hbm, qy_hbm, o1, o2, o3, qx, qy, q3, s3, v1, v2, v3, csem, osem
):
    consts = [
        pltpu.make_async_copy(qx_hbm, qx, csem.at[0]),
        pltpu.make_async_copy(qy_hbm, qy, csem.at[1]),
    ]
    for c in consts:
        c.start()
    pending = []

    def expand(t, x, v, o, nz, ny, n, order):
        done = [set() for _ in range(3)]
        rows = {0: slice(ny + 7, 2 * ny + 7), 1: slice(0, ny), 2: slice(ny + 8, 2 * ny + 8)}
        for k in order:
            value = t[k]
            lane = lax.broadcasted_iota(jnp.int32, value.shape, 1)
            first = 0.0 if x is None else roll(x[...], -(n + k))
            low = jnp.where(lane == 0, first, roll(value, 1 - n))
            planes = (low, value, roll(value, -n))
            if k < nz:
                targets = [(1, k)]
            else:
                targets = [(0, k - nz)] if k - nz < nz else []
                targets += [(2, k - nz - 1)] if k > nz else []
            for c, plane in enumerate(planes):
                plane = plane[:, 0:n]
                for a, layer in targets:
                    for b in range(3):
                        v[9 * a + 3 * b + c, layer] = plane[rows[b]]
            for a, layer in targets:
                done[a].add(layer)
                if len(done[a]) == nz:
                    part = pl.ds(9 * a, 9)
                    copy = pltpu.make_async_copy(v.at[part], o.at[part], osem.at[len(pending)])
                    copy.start()
                    pending.append(copy)

    expand(t1, x1, v1, o1, 8, 16, 64, range(17))
    expand(t2, x2, v2, o2, 4, 8, 32, range(9))

    for c in consts:
        c.wait()
    left = []
    for bx in range(4):
        blocks = [g3[4 * by + bx].reshape(32, 128) for by in range(4)]
        left += split(jnp.concatenate(blocks, axis=0))
    q3[...] = dot(jnp.concatenate(left, axis=1), qx[...])
    for h in range(2):
        rows = jnp.concatenate(
            [q3[32 * by + 16 * h:32 * by + 16 * h + 16, :] for by in range(4)], axis=0
        )
        placed = dot(qy[...], jnp.concatenate(split(rows), axis=0))
        for j in range(3):
            if 3 * h + j < 5:
                s3[3 * h + j] = placed[0:40, 128 * j:128 * j + 128]
    expand(s3, None, v3, o3, 2, 16, 64, range(5))
    for copy in pending:
        copy.wait()


def shards(coeff_z, coeff_y, coeff_x, reaction):
    vmem = pl.BlockSpec(memory_space=pltpu.VMEM)
    hbm = pl.BlockSpec(memory_space=pltpu.HBM)
    shape = jax.ShapeDtypeStruct
    v = pltpu.VMEM
    dma = pltpu.SemaphoreType.DMA
    t1, x1, t2, x2, g3 = pl.pallas_call(
        main_kernel,
        out_shape=(
            shape((17, 40, 128), F32), shape((40, 128), F32),
            shape((9, 24, 128), F32), shape((24, 128), F32),
            shape((16, 2, 16, 128), F32),
        ),
        in_specs=[hbm] * 5,
        out_specs=(vmem,) * 5,
        scratch_shapes=[
            v((4, 16, 32, 128), F32), v((576, 512), BF16),
            v((5, 32, 128), F32), v((4, 32, 128), F32), v((32, 128), F32),
            v((3, 40, 128), F32), v((3, 40, 128), F32),
            v((128, 17 * 128), BF16), v((64, 17 * 128), BF16),
            v((128, 11 * 128), BF16), v((64, 11 * 128), BF16),
            v((128, 7 * 128), BF16), v((64, 7 * 128), BF16),
            v((9, 24, 128), F32), v((5, 16, 128), F32),
            v((4, 40, 128), F32), v((2, 4, 40, 128), F32),
            v((64, 128), F32), v((2, 64, 128), F32), v((3, 64, 128), F32),
            v((4, 16, 128), F32), v((2, 16, 128), F32),
            dma((10,)), dma((12,)), dma((12,)), dma((15,)), dma((15,)),
        ],
        compiler_params=pltpu.CompilerParams(
            collective_id=0, has_side_effects=True, vmem_limit_bytes=62 << 20
        ),
    )(reaction, coeff_z, coeff_y, coeff_x, jnp.asarray(all_weights()))
    return pl.pallas_call(
        expand_kernel,
        out_shape=(
            shape((27, 8, 16, 64), F32), shape((27, 4, 8, 32), F32), shape((27, 2, 16, 64), F32),
        ),
        in_specs=[vmem] * 5 + [hbm] * 2,
        out_specs=(hbm,) * 3,
        scratch_shapes=[
            v((1024, 384), BF16), v((48, 128), BF16), v((128, 384), F32), v((5, 40, 128), F32),
            v((27, 8, 16, 64), F32), v((27, 4, 8, 32), F32), v((27, 2, 16, 64), F32),
            dma((2,)), dma((9,)),
        ],
        compiler_params=pltpu.CompilerParams(vmem_limit_bytes=62 << 20),
    )(t1, x1, t2, x2, g3, jnp.asarray(place_x(4, 16)), jnp.asarray(place_y(4, 4, 48, 16)))


def solution(mesh):
    in_specs = (P("gz", "gy", "gx"),) * 4
    out_specs = (P(None, "gz", "gy", "gx"), P(None, "gz", "gy", "gx"), P(None, "gz", None, None))
    return jax.shard_map(shards, mesh=mesh, in_specs=in_specs, out_specs=out_specs, check_vma=False)
```

```python
from functools import partial

import jax
import jax.numpy as jnp
import ml_dtypes
import numpy as np
from jax import lax
from jax.experimental import pallas as pl
from jax.experimental.pallas import tpu as pltpu
from jax.sharding import PartitionSpec as P

MESH = pl.DeviceIdType.MESH
F32 = jnp.float32
BF16 = jnp.bfloat16


def forms(level, n, last):
    step = 1 << level
    i = np.arange(n)

    def hat(i, index):
        value = np.maximum(0.0, 1.0 - np.abs(i - (step * index + step - 1)) / step)
        return np.where((i >= n) | (index >= n // step), 0.0, value) if last else value

    def slope(i, index):
        return hat(i, index) - hat(i + 1, index)

    def column(plus, index):
        other = index + plus
        return hat(i, index) * hat(i, other), slope(i, index) * slope(i, other)

    return column


def row_order(count):
    return (
        [(0, j) for j in range(count)]
        + [(1, j) for j in range(-1, count)]
        + [(0, -1), (0, count)]
    )


def y_rows(level, count):
    order = row_order(count)
    if level == 3:
        return dict(zip(order, range(len(order))))
    place = {(0, j): j for j in range(count)}
    place.update({(1, j): count + 8 + j for j in range(count)})
    place.update({(0, -1): count + 5, (0, count): count + 6, (1, -1): count + 7})
    return place


def weights_y(level, n, rows, last):
    column = forms(level, n, last)
    mass = np.zeros((rows, n))
    stiff = np.zeros((rows, n))
    for (plus, index), row in y_rows(level, n >> level).items():
        mass[row], stiff[row] = column(plus, index)
    first = np.concatenate([mass, mass, stiff, stiff], axis=1)
    second = np.concatenate([mass, mass], axis=1)
    return first, second


def lanes_of(level, n):
    count = n >> level
    if level == 3:
        return [(0, j) for j in range(-1, count + 1)] + [(1, j) for j in range(-1, count)], 128
    rim = 2 * count
    lanes = [(0, j) for j in range(count)] + [(1, j) for j in range(count)]
    lanes += [None] * (2 * count)
    lanes[rim] = (0, -1)
    lanes[rim + count // 2] = (0, count)
    lanes[rim + count] = (1, -1)
    return lanes, 4 * count


def weights_x(level, n, last):
    column = forms(level, n, last)
    lanes, width = lanes_of(level, n)
    mass = np.zeros((n, width))
    stiff = np.zeros((n, width))
    for lane, entry in enumerate(lanes):
        if entry is not None:
            mass[:, lane], stiff[:, lane] = column(*entry)
    scale = 0.5**level
    both = np.concatenate([mass, mass, stiff, stiff], axis=0) * scale
    return both


def place_x(blocks, count):
    whole = blocks * count
    out = np.zeros((blocks, 2, 128, 3 * 128))
    for block in range(blocks):
        for layer in range(3):
            entries = lanes_of(3, count * 8)[0]
            for lane, (plus, index) in enumerate(entries):
                source = 40 * layer + lane
                target = block * count + index
                if 0 <= target < whole:
                    out[block, :, source, layer * 128 + plus * whole + target] = 1.0
    return out.reshape(blocks * 256, 384).astype(ml_dtypes.bfloat16)


def place_y(blocks, count, rows, packed):
    whole = blocks * count
    out = np.zeros((rows, 2, blocks, packed))
    for block in range(blocks):
        for row, (plus, index) in enumerate(row_order(count)):
            target = block * count + index
            if 0 <= target < whole:
                out[target + plus * (whole + 8), :, block, row] = 1.0
    return out.reshape(rows, 2 * blocks * packed).astype(ml_dtypes.bfloat16)


def split(value):
    high = value.astype(BF16)
    return high, (value - high.astype(F32)).astype(BF16)


def dot(left, right):
    return jnp.dot(left, right, preferred_element_type=F32)


def roll(value, shift):
    return pltpu.roll(value, shift % 128, 1)


def mass_layers(field):
    n = len(field)
    quarter = [0.25 * field[2 * j] for j in range(n // 2)] + [None]
    same = {-1: quarter[0]}
    plus = {-1: quarter[0]}
    for j in range(n // 2):
        total = field[2 * j + 1] + quarter[j]
        same[j] = total if quarter[j + 1] is None else total + quarter[j + 1]
        plus[j] = quarter[j + 1]
    same[n // 2] = None
    return same, plus


def stiff_layers(field):
    n = len(field)
    share = {-1: 0.25 * field[0], n // 2 - 1: 0.25 * field[n - 1]}
    for j in range(n // 2 - 1):
        share[j] = 0.25 * (field[2 * j + 1] + field[2 * j + 2])
    same = {-1: share[-1], n // 2: share[n // 2 - 1]}
    for j in range(n // 2):
        same[j] = share[j - 1] + share[j]
    return same, share


def plus_of(a, b):
    if a is None:
        return b
    return a if b is None else a + b


def coarser(same, plus, count):
    def scaled(value, factor):
        return None if value is None else factor * value

    new_same, new_plus = {}, {}
    half = count // 2
    for j in range(-1, half + 1):
        total = scaled(plus_of(same.get(2 * j), same.get(2 * j + 2)), 0.25)
        for term in (same.get(2 * j + 1), plus.get(2 * j), plus.get(2 * j + 1)):
            total = plus_of(total, term)
        new_same[j] = total
    for j in range(-1, half):
        total = scaled(plus_of(plus.get(2 * j + 1), plus.get(2 * j + 2)), 0.5)
        new_plus[j] = plus_of(total, scaled(same.get(2 * j + 2), 0.25))
    return new_same, new_plus


def all_weights(last_x, last_y):
    x = np.zeros((512, 512))
    for level, start, width in ((1, 0, 256), (2, 256, 128), (3, 384, 128)):
        x[:, start:start + width] = weights_x(level, 128, last_x)
    y = np.zeros((64, 512))
    for level, row, rows, lane in ((1, 0, 48, 0), (2, 0, 32, 256), (3, 48, 16, 0)):
        first, second = weights_y(level, 32, rows, last_y)
        y[row:row + rows, lane:lane + 128] = first
        y[row:row + rows, lane + 128:lane + 192] = second
    return x.astype(ml_dtypes.bfloat16), y.astype(ml_dtypes.bfloat16)


S_PX, S_YD, S_YU, S_ROWS = 0, 64, 160, 216
R_X, R_YD, R_YU, R_D, R_ROWS = 0, 128, 224, 280, 344
Z_ONE, Z_SIDE, Z_TWO, Z_ROWS = 0, 40, 80, 104


def main_kernel(
    r_hbm, kz_hbm, ky_hbm, kx_hbm, wx_hbm, wy_hbm,
    t1, t2, own, rb, g3,
    f4, wx, wy, rims, rimr, zs, zr,
    ga1, gb1, ga2, gb2, ga3, gb3, c1, c2, c3, sb, p3,
    lsem, send, recv, gsend, grecv,
):
    gz, gy, gx = lax.axis_index("gz"), lax.axis_index("gy"), lax.axis_index("gx")
    nz, ny, nx = lax.axis_size("gz"), lax.axis_size("gy"), lax.axis_size("gx")
    zp, zm = lax.rem(gz + 1, nz), lax.rem(gz + nz - 1, nz)
    yp, ym = lax.rem(gy + 1, ny), lax.rem(gy + ny - 1, ny)
    xp, xm = lax.rem(gx + 1, nx), lax.rem(gx + nx - 1, nx)
    slab = ny * nx
    me = gy * nx + gx
    peers = []
    for d in range(1, slab):
        t = lax.rem(me + d, slab)
        peers.append((gz, lax.div(t, nx), lax.rem(t, nx)))

    barrier = pltpu.get_barrier_semaphore()
    others = [(zp, gy, gx), (zm, gy, gx)]
    for device in others + peers:
        pl.semaphore_signal(barrier, inc=1, device_id=device, device_id_type=MESH)

    end_x = jnp.where(gx == nx - 1, 1, 0)
    end_y = jnp.where(gy == ny - 1, 1, 0)
    loads = [
        pltpu.make_async_copy(f, f4.at[j], lsem.at[j])
        for j, f in enumerate((r_hbm, kz_hbm, ky_hbm, kx_hbm))
    ]
    loads.append(pltpu.make_async_copy(wx_hbm.at[end_x], wx, lsem.at[4]))
    loads.append(pltpu.make_async_copy(wy_hbm.at[end_y], wy, lsem.at[5]))
    for c in loads:
        c.start()

    started = []

    def copy(src, dst, device):
        k = len(started)
        c = pltpu.make_async_remote_copy(
            src_ref=src, dst_ref=dst, send_sem=send.at[k], recv_sem=recv.at[k],
            device_id=device, device_id_type=MESH,
        )
        c.start()
        started.append(c)
        return c

    for c in loads:
        c.wait()

    def layers(j):
        return [f4[j, k] for k in range(16)]

    same1, plus1 = mass_layers(layers(0))
    ssame, share = stiff_layers(layers(1))
    for j in range(-1, 9):
        same1[j] = plus_of(same1[j], ssame[j])
    for j in range(-1, 8):
        plus1[j] = -share[j] if plus1[j] is None else plus1[j] - share[j]
    level1 = [(same1, plus1), mass_layers(layers(2)), mass_layers(layers(3))]
    level2 = [coarser(*f, 8) for f in level1]
    level3 = [coarser(*f, 4) for f in level2]
    top_z, low_z = gz == nz - 1, gz == 0
    for level, n, factor in ((level1, 8, 3.0), (level2, 4, 15.0), (level3, 2, 63.0)):
        same, plus = level[0]
        last = jnp.where(top_z, same[n], 0.0)
        same[n - 1] = same[n - 1] + factor * last
        plus[n - 1] = plus[n - 1] + last

    zero = jnp.zeros((32, 128), F32)

    def put(ga, gb, j, values):
        lanes = pl.ds(128 * j, 128)
        for base, (ref, value) in enumerate(zip((ga, ga, gb), values)):
            high, low = split(zero if value is None else value)
            start = 64 * base if base < 2 else 0
            ref[start:start + 32, lanes] = high
            ref[start + 32:start + 64, lanes] = low

    def reduce_yx(level, count, ga, gb, wya, wyb, wxl, rows):
        order = row_order(count)
        for j, (plus, index) in enumerate(order):
            put(ga, gb, j, [f[plus][index] for f in level])
        left = []
        for value in (dot(wya, ga[...]), dot(wyb, gb[...])):
            stacked = jnp.concatenate(
                [value[:, 128 * j:128 * j + 128] for j in range(len(order))], axis=0
            )
            left += split(stacked)
        out = dot(jnp.concatenate(left, axis=1), wxl)
        return [out[rows * j:rows * j + rows] for j in range(len(order))]

    out3 = reduce_yx(
        level3, 2, ga3, gb3, wy[48:64, 0:128], wy[48:64, 128:192], wx[:, 384:512], 16
    )
    for k, j in enumerate((5, 2, 6)):
        rims[16 * k:16 * k + 16] = out3[j]
    for j in range(5):
        c3[j] = out3[j]
    pl.semaphore_wait(barrier, slab - 1 + len(others))
    round_z = [
        copy(rims.at[0:32], rimr.at[0:32], (zm, gy, gx)),
        copy(rims.at[32:48], rimr.at[32:48], (zp, gy, gx)),
    ]

    out2 = reduce_yx(
        level2, 4, ga2, gb2, wy[0:32, 256:384], wy[0:32, 384:448], wx[:, 256:384], 32
    )
    out2 = [value[0:24] for value in out2]
    out1 = reduce_yx(
        level1, 8, ga1, gb1, wy[0:48, 0:128], wy[0:48, 128:192], wx[:, 0:256], 48
    )
    side1 = [value[0:40, 128:256] for value in out1]
    out1 = [value[0:40, 0:128] for value in out1]
    for k, (one, two) in enumerate(((17, 9), (8, 4), (18, 10))):
        start = Z_ROWS * k
        zs[start + Z_ONE:start + Z_ONE + 40] = out1[one]
        zs[start + Z_SIDE:start + Z_SIDE + 40] = side1[one]
        zs[start + Z_TWO:start + Z_TWO + 24] = out2[two]
    faces = [
        copy(zs.at[pl.ds(0, 2 * Z_ROWS)], zr.at[pl.ds(0, 2 * Z_ROWS)], (zm, gy, gx)),
        copy(zs.at[pl.ds(2 * Z_ROWS, Z_ROWS)], zr.at[pl.ds(2 * Z_ROWS, Z_ROWS)], (zp, gy, gx)),
    ]

    lane2 = lax.broadcasted_iota(jnp.int32, (24, 128), 1)
    totals = [None, None]

    def pack(k, one, side, two):
        if one is not None:
            c1[k] = one
            totals[0] = plus_of(totals[0], roll(side, k) if k else side)
            for start, row in ((S_YD, 21), (S_YD + 40, 23), (S_YU + 16, 22)):
                sb[start + k:start + k + 1] = one[row:row + 1]
        if two is not None:
            c2[k] = two
            totals[1] = plus_of(
                totals[1], roll(jnp.where(lane2 >= 64, two, 0.0), 64 + k)
            )
            for start, row in ((S_YD, 13), (S_YD + 40, 15), (S_YU + 16, 14)):
                sb[start + 24 + k:start + 25 + k] = two[row:row + 1]

    blank = jnp.zeros((40, 128), F32)
    for start in (S_YD, S_YD + 40, S_YU + 16):
        sb[start:start + 40] = blank
    for k in range(17):
        if k not in (0, 7, 8, 16):
            pack(k, out1[k], side1[k], None)
    for k in range(9):
        if k not in (0, 3, 4, 8):
            pack(k, None, None, out2[k])

    for c in round_z:
        c.wait_recv()
    low = jnp.where(low_z, 0.0, rimr[32:48])
    fix3 = {
        0: low, 1: jnp.where(top_z, 0.0, rimr[0:16]),
        2: -low, 4: jnp.where(top_z, 0.0, rimr[16:32]),
    }
    packed = [None, None]
    for j in range(5):
        value = c3[j] if j not in fix3 else c3[j] + fix3[j]
        if j == 2:
            value = jnp.where(low_z, 0.0, value)
        packed[j // 3] = plus_of(packed[j // 3], roll(value, 40 * (j % 3)) if j % 3 else value)
    p3[0] = packed[0]
    p3[1] = packed[1]
    gather = []
    for d, device in enumerate(peers):
        c = pltpu.make_async_remote_copy(
            src_ref=p3, dst_ref=g3.at[me], send_sem=gsend.at[d], recv_sem=grecv.at[d],
            device_id=device, device_id_type=MESH,
        )
        c.start()
        gather.append(c)
    mine = pltpu.make_async_copy(p3, g3.at[me], lsem.at[3])
    mine.start()

    for c in faces:
        c.wait_recv()

    def came(k, start, rows):
        value = zr[Z_ROWS * k + start:Z_ROWS * k + start + rows]
        return jnp.where(low_z if k == 2 else top_z, 0.0, value)

    def fixed(values, n, start, rows):
        low = came(2, start, rows)
        return {
            0: values[0] + low,
            n - 1: values[n - 1] + came(0, start, rows),
            n: jnp.where(low_z, 0.0, values[n] - low),
            2 * n: values[2 * n] + came(1, start, rows),
        }

    one, side = fixed(out1, 8, Z_ONE, 40), fixed(side1, 8, Z_SIDE, 40)
    for k in one:
        pack(k, one[k], side[k], None)
    for k, value in fixed(out2, 4, Z_TWO, 24).items():
        pack(k, None, None, value)
    total1, total2 = totals
    sb[S_PX:S_PX + 16] = total1[0:16]
    sb[S_PX + 16:S_PX + 32] = total1[24:40]
    sb[S_PX + 32:S_PX + 40] = total2[0:8]
    sb[S_PX + 40:S_PX + 48] = total2[16:24]
    for start in (S_PX + 48, S_YD + 80, S_YU):
        sb[start:start + 8] = total1[16:24]
        sb[start + 8:start + 16] = total2[8:16]
    y_to, x_to = (ym, yp), (xm, xp)
    for yi in range(2):
        for xi in range(2):
            k = 16 * (2 * yi + xi)
            copy(
                sb.at[pl.ds(S_PX + 48, 16)], rb.at[pl.ds(R_D + k, 16)], (gz, y_to[yi], x_to[xi])
            )
    for k in range(2):
        copy(sb.at[pl.ds(S_PX, 64)], rb.at[pl.ds(R_X + 64 * k, 64)], (gz, gy, x_to[k]))
    copy(sb.at[pl.ds(S_YD, 96)], rb.at[pl.ds(R_YD, 96)], (gz, ym, gx))
    copy(sb.at[pl.ds(S_YU, 56)], rb.at[pl.ds(R_YU, 56)], (gz, yp, gx))

    stores = [
        pltpu.make_async_copy(c1, t1, lsem.at[0]),
        pltpu.make_async_copy(c2, t2, lsem.at[1]),
        pltpu.make_async_copy(sb.at[pl.ds(S_PX, 64)], own, lsem.at[2]),
    ]
    for c in stores:
        c.start()
    for c in stores:
        c.wait()
    mine.wait()
    for c in started[4:]:
        c.wait_recv()
    for c in gather:
        c.wait()
    for c in started:
        c.wait_send()


def finish_kernel(
    t1_hbm, t2_hbm, own_hbm, rb_hbm, g3_hbm, qx_hbm, qy_hbm, o1, o2, o3,
    t1, t2, px, rb, g3, qx, qy, x1, x2, q3, s3, v1, v2, v3, csem, osem,
):
    gy, gx = lax.axis_index("gy"), lax.axis_index("gx")
    ny, nx = lax.axis_size("gy"), lax.axis_size("gx")
    loads = [
        pltpu.make_async_copy(src, dst, csem.at[k])
        for k, (src, dst) in enumerate((
            (rb_hbm, rb), (t1_hbm, t1), (t2_hbm, t2), (own_hbm, px.at[0]),
            (g3_hbm, g3), (qx_hbm, qx), (qy_hbm, qy),
        ))
    ]
    for c in loads:
        c.start()

    def present(flag):
        return jnp.where(flag, 1.0, 0.0).astype(F32)

    from_up_y, from_low_y = present(gy < ny - 1), present(gy > 0)
    from_up_x, from_low_x = present(gx < nx - 1), present(gx > 0)
    for c in loads[0:4]:
        c.wait()

    for k in range(2):
        px[1 + k] = rb[R_X + 64 * k:R_X + 64 * k + 64]
    side = [(rb[R_YD + 80:R_YD + 96], rb[R_YU:R_YU + 16])]
    for xi in range(2):
        side.append(tuple(rb[R_D + 16 * k:R_D + 16 * k + 16] for k in (xi, 2 + xi)))
    for k, (upper, lower) in enumerate(side):
        upper, lower = from_up_y * upper, from_low_y * lower
        for same, plus, rim, group in ((0, 16, 48, 0), (32, 40, 56, 8)):
            n = plus - same
            for row, value in (
                (same + n - 1, upper[group + 5:group + 6]),
                (plus + n - 1, upper[group + 7:group + 8]),
                (same, lower[group + 6:group + 7]),
            ):
                px[k, row:row + 1] = px[k, row:row + 1] + value
            row = rim + 7
            px[k, row:row + 1] = (px[k, row:row + 1] - lower[group + 6:group + 7]) * from_low_y

    sets = (
        (t1, x1, 8, 16, 64, (0, 16, 48), 0),
        (t2, x2, 4, 8, 32, (32, 40, 56), 24),
    )
    for t, x, lz, n, lanes, parts, rows_at in sets:
        count = 2 * lz + 1
        size = 24 if n == 16 else 16
        same_up = from_up_y * rb[R_YD + rows_at:R_YD + rows_at + size]
        plus_up = from_up_y * rb[R_YD + 40 + rows_at:R_YD + 40 + rows_at + size]
        low = from_low_y * rb[R_YU + 16 + rows_at:R_YU + 16 + rows_at + size]
        for j in range(count):
            t[j, n - 1:n] = t[j, n - 1:n] + same_up[j:j + 1]
            t[j, 2 * n + 7:2 * n + 8] = t[j, 2 * n + 7:2 * n + 8] + plus_up[j:j + 1]
            t[j, 0:1] = t[j, 0:1] + low[j:j + 1]
            t[j, n + 7:n + 8] = (t[j, n + 7:n + 8] - low[j:j + 1]) * from_low_y

        def column(k):
            same, plus, rim = (px[k, s:s + z] for s, z in zip(parts, (n, n, 8)))
            return jnp.concatenate([same, rim, plus], axis=0)

        above, below = from_up_x * column(1), from_low_x * column(2)
        x[...] = (column(0) - roll(below, lanes // 2)) * from_low_x
        lane = lax.broadcasted_iota(jnp.int32, above.shape, 1)
        at_end = (lane == lanes - 1) | (lane == 2 * lanes - 1)
        for j in range(count):
            value = t[j] + jnp.where(at_end, roll(above, lanes - 1 - j), 0.0)
            t[j] = value + jnp.where(lane == 0, roll(below, -(lanes // 2) - j), 0.0)

    pending = []

    def expand(t, x, v, o, nz, ny, n):
        done = [set() for _ in range(3)]
        rows = {0: slice(ny + 7, 2 * ny + 7), 1: slice(0, ny), 2: slice(ny + 8, 2 * ny + 8)}
        for k in range(2 * nz + 1):
            value = t[k]
            first = 0.0 if x is None else roll(x[...], -(n + k))
            lane = lax.broadcasted_iota(jnp.int32, value.shape, 1)
            low = jnp.where(lane == 0, first, roll(value, 1 - n))
            planes = (low, value, roll(value, -n))
            if k < nz:
                targets = [(1, k)]
            else:
                targets = [(0, k - nz)] if k - nz < nz else []
                targets += [(2, k - nz - 1)] if k > nz else []
            for c, plane in enumerate(planes):
                plane = plane[:, 0:n]
                for a, layer in targets:
                    for b in range(3):
                        v[9 * a + 3 * b + c, layer] = plane[rows[b]]
            for a, layer in targets:
                done[a].add(layer)
                if len(done[a]) == nz:
                    part = pl.ds(9 * a, 9)
                    copy = pltpu.make_async_copy(v.at[part], o.at[part], osem.at[len(pending)])
                    copy.start()
                    pending.append(copy)

    expand(t1, x1, v1, o1, 8, 16, 64)
    expand(t2, x2, v2, o2, 4, 8, 32)

    for c in loads[4:]:
        c.wait()
    left = []
    for bx in range(4):
        blocks = [g3[4 * by + bx].reshape(32, 128) for by in range(4)]
        left += split(jnp.concatenate(blocks, axis=0))
    q3[...] = dot(jnp.concatenate(left, axis=1), qx[...])
    for h in range(2):
        rows = jnp.concatenate(
            [q3[32 * by + 16 * h:32 * by + 16 * h + 16, :] for by in range(4)], axis=0
        )
        placed = dot(qy[...], jnp.concatenate(split(rows), axis=0))
        for j in range(3):
            if 3 * h + j < 5:
                s3[3 * h + j] = placed[0:40, 128 * j:128 * j + 128]
    expand(s3, None, v3, o3, 2, 16, 64)
    for copy in pending:
        copy.wait()


def shards(coeff_z, coeff_y, coeff_x, reaction):
    hbm = pl.BlockSpec(memory_space=pltpu.HBM)
    shape = jax.ShapeDtypeStruct
    v = pltpu.VMEM
    dma = pltpu.SemaphoreType.DMA
    pairs = [all_weights(flag, flag) for flag in (False, True)]
    wx, wy = (jnp.asarray(np.stack([pair[k] for pair in pairs])) for k in range(2))
    between = (
        shape((17, 40, 128), F32), shape((9, 24, 128), F32), shape((64, 128), F32),
        shape((R_ROWS, 128), F32), shape((16, 2, 16, 128), F32),
    )
    middle = pl.pallas_call(
        main_kernel,
        out_shape=between,
        in_specs=[hbm] * 6,
        out_specs=(hbm,) * 5,
        scratch_shapes=[
            v((4, 16, 32, 128), F32), v((512, 512), BF16), v((64, 512), BF16),
            v((48, 128), F32), v((48, 128), F32),
            v((3 * Z_ROWS, 128), F32), v((3 * Z_ROWS, 128), F32),
            v((128, 19 * 128), BF16), v((64, 19 * 128), BF16),
            v((128, 11 * 128), BF16), v((64, 11 * 128), BF16),
            v((128, 7 * 128), BF16), v((64, 7 * 128), BF16),
            v((17, 40, 128), F32), v((9, 24, 128), F32), v((5, 16, 128), F32),
            v((S_ROWS, 128), F32), v((2, 16, 128), F32),
            dma((6,)), dma((12,)), dma((12,)), dma((15,)), dma((15,)),
        ],
        compiler_params=pltpu.CompilerParams(
            collective_id=0, has_side_effects=True, vmem_limit_bytes=62 << 20
        ),
    )(reaction, coeff_z, coeff_y, coeff_x, wx, wy)
    return pl.pallas_call(
        finish_kernel,
        out_shape=(
            shape((27, 8, 16, 64), F32), shape((27, 4, 8, 32), F32), shape((27, 2, 16, 64), F32),
        ),
        in_specs=[hbm] * 7,
        out_specs=(hbm,) * 3,
        scratch_shapes=[
            v((17, 40, 128), F32), v((9, 24, 128), F32), v((3, 64, 128), F32),
            v((R_ROWS, 128), F32), v((16, 2, 16, 128), F32),
            v((1024, 384), BF16), v((48, 128), BF16), v((40, 128), F32), v((24, 128), F32),
            v((128, 384), F32), v((5, 40, 128), F32),
            v((27, 8, 16, 64), F32), v((27, 4, 8, 32), F32), v((27, 2, 16, 64), F32),
            dma((7,)), dma((9,)),
        ],
        compiler_params=pltpu.CompilerParams(vmem_limit_bytes=62 << 20),
    )(*middle, jnp.asarray(place_x(4, 16)), jnp.asarray(place_y(4, 4, 48, 16)))


def solution(mesh):
    in_specs = (P("gz", "gy", "gx"),) * 4
    out_specs = (P(None, "gz", "gy", "gx"), P(None, "gz", "gy", "gx"), P(None, "gz", None, None))
    return jax.shard_map(shards, mesh=mesh, in_specs=in_specs, out_specs=out_specs, check_vma=False)
```

```python
from functools import partial

import jax
import jax.numpy as jnp
import ml_dtypes
import numpy as np
from jax import lax
from jax.experimental import pallas as pl
from jax.experimental.pallas import tpu as pltpu
from jax.sharding import PartitionSpec as P

MESH = pl.DeviceIdType.MESH
F32 = jnp.float32
BF16 = jnp.bfloat16


def forms(level, n, last):
    step = 1 << level
    i = np.arange(n)

    def hat(i, index):
        value = np.maximum(0.0, 1.0 - np.abs(i - (step * index + step - 1)) / step)
        return np.where((i >= n) | (index >= n // step), 0.0, value) if last else value

    def slope(i, index):
        return hat(i, index) - hat(i + 1, index)

    def column(plus, index):
        other = index + plus
        return hat(i, index) * hat(i, other), slope(i, index) * slope(i, other)

    return column


def row_order(count):
    return (
        [(0, j) for j in range(count)]
        + [(1, j) for j in range(-1, count)]
        + [(0, -1), (0, count)]
    )


def y_rows(level, count):
    order = row_order(count)
    if level == 3:
        return dict(zip(order, range(len(order))))
    place = {(0, j): j for j in range(count)}
    place.update({(1, j): count + 8 + j for j in range(count)})
    place.update({(0, -1): count + 5, (0, count): count + 6, (1, -1): count + 7})
    return place


def weights_y(level, n, rows, last):
    column = forms(level, n, last)
    mass = np.zeros((rows, n))
    stiff = np.zeros((rows, n))
    for (plus, index), row in y_rows(level, n >> level).items():
        mass[row], stiff[row] = column(plus, index)
    first = np.concatenate([mass, mass, stiff, stiff], axis=1)
    second = np.concatenate([mass, mass], axis=1)
    return first, second


def lanes_of(level, n):
    count = n >> level
    if level == 3:
        return [(0, j) for j in range(-1, count + 1)] + [(1, j) for j in range(-1, count)], 128
    rim = 2 * count
    lanes = [(0, j) for j in range(count)] + [(1, j) for j in range(count)]
    lanes += [None] * (2 * count)
    lanes[rim] = (0, -1)
    lanes[rim + count // 2] = (0, count)
    lanes[rim + count] = (1, -1)
    return lanes, 4 * count


def weights_x(level, n, last):
    column = forms(level, n, last)
    lanes, width = lanes_of(level, n)
    mass = np.zeros((n, width))
    stiff = np.zeros((n, width))
    for lane, entry in enumerate(lanes):
        if entry is not None:
            mass[:, lane], stiff[:, lane] = column(*entry)
    scale = 0.5**level
    both = np.concatenate([mass, mass, stiff, stiff], axis=0) * scale
    return both


def place_x(count):
    out = np.zeros((2, 128, 3 * 128))
    for layer in range(3):
        for lane, (plus, index) in enumerate(lanes_of(3, count * 8)[0]):
            out[:, 40 * layer + lane, layer * 128 + plus * 64 + count + index] = 1.0
    return out.reshape(256, 384).astype(ml_dtypes.bfloat16)


def place_y(blocks, count, rows, packed, shift):
    whole = blocks * count
    out = np.zeros((rows, 2, blocks, packed))
    for block in range(blocks):
        for row, (plus, index) in enumerate(row_order(count)):
            target = block * count + index
            if 0 <= target < whole:
                out[target + plus * (whole + 8), :, block, row + shift] = 1.0
    return out.reshape(rows, 2 * blocks * packed).astype(ml_dtypes.bfloat16)


def split(value):
    high = value.astype(BF16)
    return high, (value - high.astype(F32)).astype(BF16)


def dot(left, right):
    return jnp.dot(left, right, preferred_element_type=F32)


def roll(value, shift):
    return pltpu.roll(value, shift % 128, 1)


def mass_layers(field):
    n = len(field)
    quarter = [0.25 * field[2 * j] for j in range(n // 2)] + [None]
    same = {-1: quarter[0]}
    plus = {-1: quarter[0]}
    for j in range(n // 2):
        total = field[2 * j + 1] + quarter[j]
        same[j] = total if quarter[j + 1] is None else total + quarter[j + 1]
        plus[j] = quarter[j + 1]
    same[n // 2] = None
    return same, plus


def stiff_layers(field):
    n = len(field)
    share = {-1: 0.25 * field[0], n // 2 - 1: 0.25 * field[n - 1]}
    for j in range(n // 2 - 1):
        share[j] = 0.25 * (field[2 * j + 1] + field[2 * j + 2])
    same = {-1: share[-1], n // 2: share[n // 2 - 1]}
    for j in range(n // 2):
        same[j] = share[j - 1] + share[j]
    return same, share


def plus_of(a, b):
    if a is None:
        return b
    return a if b is None else a + b


def coarser(same, plus, count):
    def scaled(value, factor):
        return None if value is None else factor * value

    new_same, new_plus = {}, {}
    half = count // 2
    for j in range(-1, half + 1):
        total = scaled(plus_of(same.get(2 * j), same.get(2 * j + 2)), 0.25)
        for term in (same.get(2 * j + 1), plus.get(2 * j), plus.get(2 * j + 1)):
            total = plus_of(total, term)
        new_same[j] = total
    for j in range(-1, half):
        total = scaled(plus_of(plus.get(2 * j + 1), plus.get(2 * j + 2)), 0.5)
        new_plus[j] = plus_of(total, scaled(same.get(2 * j + 2), 0.25))
    return new_same, new_plus


def all_weights(last_x, last_y):
    x = np.zeros((512, 512))
    for level, start, width in ((1, 0, 256), (2, 256, 128), (3, 384, 128)):
        x[:, start:start + width] = weights_x(level, 128, last_x)
    y = np.zeros((64, 512))
    for level, row, rows, lane in ((1, 0, 48, 0), (2, 0, 32, 256), (3, 48, 16, 0)):
        first, second = weights_y(level, 32, rows, last_y)
        y[row:row + rows, lane:lane + 128] = first
        y[row:row + rows, lane + 128:lane + 192] = second
    return x.astype(ml_dtypes.bfloat16), y.astype(ml_dtypes.bfloat16)


S_PX, S_YD, S_YU, S_ROWS = 0, 64, 144, 192
R_X, R_YD, R_YU, R_D, R_ROWS = 0, 128, 208, 256, 320
Z_ONE, Z_TWO, Z_THREE, Z_ROWS = 0, 40, 64, 80


def main_kernel(
    r_hbm, kz_hbm, ky_hbm, kx_hbm, wx_hbm, wy_hbm,
    t1, t2, own, rb, g3,
    f4, wx, wy, zs, zr,
    gaf, gbf, ga1, gb1, ga2, gb2, ga3, gb3, c1, c2, c3, sb, p3,
    lsem, send, recv, gsend, grecv,
):
    gz, gy, gx = lax.axis_index("gz"), lax.axis_index("gy"), lax.axis_index("gx")
    nz, ny, nx = lax.axis_size("gz"), lax.axis_size("gy"), lax.axis_size("gx")
    zp, zm = lax.rem(gz + 1, nz), lax.rem(gz + nz - 1, nz)
    yp, ym = lax.rem(gy + 1, ny), lax.rem(gy + ny - 1, ny)
    xp, xm = lax.rem(gx + 1, nx), lax.rem(gx + nx - 1, nx)
    slab = ny * nx
    me = gy * nx + gx
    offsets = [(dy, dx) for dx in (2, 1, 3, 0) for dy in (2, 1, 3, 0) if dy or dx]
    peers = [(gz, lax.rem(gy + dy, ny), lax.rem(gx + dx, nx)) for dy, dx in offsets]

    barrier = pltpu.get_barrier_semaphore()
    others = [(zp, gy, gx), (zm, gy, gx)]
    for device in others + peers:
        pl.semaphore_signal(barrier, inc=1, device_id=device, device_id_type=MESH)

    end_x = jnp.where(gx == nx - 1, 1, 0)
    end_y = jnp.where(gy == ny - 1, 1, 0)
    loads = [
        pltpu.make_async_copy(f, f4.at[j], lsem.at[j])
        for j, f in enumerate((r_hbm, kz_hbm, ky_hbm, kx_hbm))
    ]
    loads.append(pltpu.make_async_copy(wx_hbm.at[end_x], wx, lsem.at[4]))
    loads.append(pltpu.make_async_copy(wy_hbm.at[end_y], wy, lsem.at[5]))
    for c in loads:
        c.start()

    started = []

    def copy(src, dst, device):
        k = len(started)
        c = pltpu.make_async_remote_copy(
            src_ref=src, dst_ref=dst, send_sem=send.at[k], recv_sem=recv.at[k],
            device_id=device, device_id_type=MESH,
        )
        c.start()
        started.append(c)
        return c

    for c in loads:
        c.wait()

    def layers(j):
        return [f4[j, k] for k in range(16)]

    same1, plus1 = mass_layers(layers(0))
    ssame, share = stiff_layers(layers(1))
    for j in range(-1, 9):
        same1[j] = plus_of(same1[j], ssame[j])
    for j in range(-1, 8):
        plus1[j] = -share[j] if plus1[j] is None else plus1[j] - share[j]
    level1 = [(same1, plus1), mass_layers(layers(2)), mass_layers(layers(3))]
    level2 = [coarser(*f, 8) for f in level1]
    level3 = [coarser(*f, 4) for f in level2]
    top_z, low_z = gz == nz - 1, gz == 0
    for level, n, factor in ((level1, 8, 3.0), (level2, 4, 15.0), (level3, 2, 63.0)):
        same, plus = level[0]
        last = jnp.where(top_z, same[n], 0.0)
        same[n - 1] = same[n - 1] + factor * last
        plus[n - 1] = plus[n - 1] + last

    zero = jnp.zeros((32, 128), F32)

    def put(ga, gb, j, values):
        lanes = pl.ds(128 * j, 128)
        for base, (ref, value) in enumerate(zip((ga, ga, gb), values)):
            high, low = split(zero if value is None else value)
            start = 64 * base if base < 2 else 0
            ref[start:start + 32, lanes] = high
            ref[start + 32:start + 64, lanes] = low

    def reduce_yx(level, count, places, ga, gb, wya, wyb, wxl, rows):
        order = row_order(count)
        for j, k in enumerate(places):
            plus, index = order[k]
            put(ga, gb, j, [f[plus][index] for f in level])
        size = len(places)
        left = []
        for value in (dot(wya, ga[:, 0:128 * size]), dot(wyb, gb[:, 0:128 * size])):
            stacked = jnp.concatenate(
                [value[:, 128 * j:128 * j + 128] for j in range(size)], axis=0
            )
            left += split(stacked)
        out = dot(jnp.concatenate(left, axis=1), wxl)
        return {k: out[rows * j:rows * j + rows] for j, k in enumerate(places)}

    def reduce_one(places, ga, gb):
        out = reduce_yx(
            level1, 8, places, ga, gb, wy[0:48, 0:128], wy[0:48, 128:192], wx[:, 0:256], 48
        )
        for k, value in out.items():
            side1[k] = value[0:40, 128:256]
            out1[k] = value[0:40, 0:128]

    out3 = reduce_yx(
        level3, 2, range(7), ga3, gb3, wy[48:64, 0:128], wy[48:64, 128:192], wx[:, 384:512], 16
    )
    out2 = reduce_yx(
        level2, 4, range(11), ga2, gb2, wy[0:32, 256:384], wy[0:32, 384:448], wx[:, 256:384], 32
    )
    out2 = {k: value[0:24] for k, value in out2.items()}
    out1, side1 = {}, {}
    reduce_one((8, 17, 18), gaf, gbf)
    lane1 = lax.broadcasted_iota(jnp.int32, (40, 128), 1)
    low_pair, high_one = (lane1 == 65) | (lane1 == 97), lane1 == 69
    for k, (one, two, three) in enumerate(((17, 9, 5), (8, 4, 2), (18, 10, 6))):
        start = Z_ROWS * k
        zs[start + Z_ONE:start + Z_ONE + 40] = out1[one]
        rest = jnp.concatenate([out2[two], out3[three]], axis=0)
        rest = jnp.where(low_pair, roll(side1[one], 65), rest)
        zs[start + Z_TWO:start + Z_ROWS] = jnp.where(high_one, roll(side1[one], 5), rest)
    for j in range(5):
        c3[j] = out3[j]
    pl.semaphore_wait(barrier, slab - 1 + len(others))
    faces = [
        copy(zs.at[pl.ds(0, 2 * Z_ROWS)], zr.at[pl.ds(0, 2 * Z_ROWS)], (zm, gy, gx)),
        copy(zs.at[pl.ds(2 * Z_ROWS, Z_ROWS)], zr.at[pl.ds(2 * Z_ROWS, Z_ROWS)], (zp, gy, gx)),
    ]
    reduce_one(tuple(range(8)) + tuple(range(9, 17)), ga1, gb1)

    lane2 = lax.broadcasted_iota(jnp.int32, (24, 128), 1)
    totals = [None, None]

    def pack(k, one, side, two):
        if one is not None:
            c1[k] = one
            totals[0] = plus_of(totals[0], roll(side, k) if k else side)
            for start, row in ((S_YD, 21), (S_YD + 32, 23), (S_YU + 16, 22)):
                sb[start + k:start + k + 1] = one[row:row + 1]
        if two is not None:
            c2[k] = two
            totals[1] = plus_of(
                totals[1], roll(jnp.where(lane2 >= 64, two, 0.0), 64 + k)
            )
            for start, row in ((S_YD, 13), (S_YD + 32, 15), (S_YU + 16, 14)):
                sb[start + 17 + k:start + 18 + k] = two[row:row + 1]

    blank = jnp.zeros((32, 128), F32)
    for start in (S_YD, S_YD + 32, S_YU + 16):
        sb[start:start + 32] = blank
    for k in range(17):
        if k not in (0, 7, 8, 16):
            pack(k, out1[k], side1[k], None)
    for k in range(9):
        if k not in (0, 3, 4, 8):
            pack(k, None, None, out2[k])

    for c in faces:
        c.wait_recv()

    def came(k, start, rows):
        value = zr[Z_ROWS * k + start:Z_ROWS * k + start + rows]
        return jnp.where(low_z if k == 2 else top_z, 0.0, value)

    lane3 = lax.broadcasted_iota(jnp.int32, (16, 128), 1)
    down0, down1, low = (jnp.where(lane3 < 40, came(k, Z_THREE, 16), 0.0) for k in range(3))
    fix3 = {0: low, 1: down0, 2: -low, 4: down1}
    packed = [None, None]
    for j in range(5):
        value = c3[j] if j not in fix3 else c3[j] + fix3[j]
        if j == 2:
            value = jnp.where(low_z, 0.0, value)
        packed[j // 3] = plus_of(packed[j // 3], roll(value, 40 * (j % 3)) if j % 3 else value)
    p3[0:16] = packed[0]
    p3[12:24] = packed[1][0:12]
    gather = []
    for d, device in enumerate(peers):
        c = pltpu.make_async_remote_copy(
            src_ref=p3, dst_ref=g3.at[me], send_sem=gsend.at[d], recv_sem=grecv.at[d],
            device_id=device, device_id_type=MESH,
        )
        c.start()
        gather.append(c)
    mine = pltpu.make_async_copy(p3, g3.at[me], lsem.at[3])
    mine.start()

    def came_side(k):
        value = came(k, Z_TWO, 40)
        return roll(jnp.where(low_pair, value, 0.0), -65) + roll(jnp.where(high_one, value, 0.0), -5)

    def came_two(k):
        value = came(k, Z_TWO, 24)
        return jnp.where((lane2 == 65) | (lane2 == 97) | (lane2 == 69), 0.0, value)

    def fixed(values, n, part):
        low = part(2)
        return {
            0: values[0] + low,
            n - 1: values[n - 1] + part(0),
            n: jnp.where(low_z, 0.0, values[n] - low),
            2 * n: values[2 * n] + part(1),
        }

    one, side = fixed(out1, 8, lambda k: came(k, Z_ONE, 40)), fixed(side1, 8, came_side)
    for k in one:
        pack(k, one[k], side[k], None)
    for k, value in fixed(out2, 4, came_two).items():
        pack(k, None, None, value)
    total1, total2 = totals
    sb[S_PX:S_PX + 16] = total1[0:16]
    sb[S_PX + 16:S_PX + 32] = total1[24:40]
    sb[S_PX + 32:S_PX + 40] = total2[0:8]
    sb[S_PX + 40:S_PX + 48] = total2[16:24]
    for start in (S_PX + 48, S_YD + 64, S_YU):
        sb[start:start + 8] = total1[16:24]
        sb[start + 8:start + 16] = total2[8:16]
    y_to, x_to = (ym, yp), (xm, xp)
    for yi in range(2):
        for xi in range(2):
            k = 16 * (2 * yi + xi)
            copy(
                sb.at[pl.ds(S_PX + 48, 16)], rb.at[pl.ds(R_D + k, 16)], (gz, y_to[yi], x_to[xi])
            )
    for k in range(2):
        copy(sb.at[pl.ds(S_PX, 64)], rb.at[pl.ds(R_X + 64 * k, 64)], (gz, gy, x_to[k]))
    copy(sb.at[pl.ds(S_YD, 80)], rb.at[pl.ds(R_YD, 80)], (gz, ym, gx))
    copy(sb.at[pl.ds(S_YU, 48)], rb.at[pl.ds(R_YU, 48)], (gz, yp, gx))

    stores = [
        pltpu.make_async_copy(c1, t1, lsem.at[0]),
        pltpu.make_async_copy(c2, t2, lsem.at[1]),
        pltpu.make_async_copy(sb.at[pl.ds(S_PX, 64)], own, lsem.at[2]),
    ]
    for c in stores:
        c.start()
    for c in stores:
        c.wait()
    mine.wait()
    for c in started[2:]:
        c.wait_recv()
    for c in gather:
        c.wait()
    for c in started:
        c.wait_send()


def finish_kernel(
    t1_hbm, t2_hbm, own_hbm, rb_hbm, g3_hbm, qx_hbm, qy_hbm, o1, o2, o3,
    t1, t2, px, rb, g3, qx, qy, x1, x2, q3, s3, v1, v2, v3, csem, osem,
):
    gy, gx = lax.axis_index("gy"), lax.axis_index("gx")
    ny, nx = lax.axis_size("gy"), lax.axis_size("gx")
    loads = [
        pltpu.make_async_copy(src, dst, csem.at[k])
        for k, (src, dst) in enumerate((
            (rb_hbm, rb), (t1_hbm, t1), (t2_hbm, t2), (own_hbm, px.at[0]),
            (g3_hbm, g3), (qx_hbm, qx), (qy_hbm, qy),
        ))
    ]
    for c in loads:
        c.start()

    def present(flag):
        return jnp.where(flag, 1.0, 0.0).astype(F32)

    from_up_y, from_low_y = present(gy < ny - 1), present(gy > 0)
    from_up_x, from_low_x = present(gx < nx - 1), present(gx > 0)
    for c in loads[0:4]:
        c.wait()

    for k in range(2):
        px[1 + k] = rb[R_X + 64 * k:R_X + 64 * k + 64]
    side = [(rb[R_YD + 64:R_YD + 80], rb[R_YU:R_YU + 16])]
    for xi in range(2):
        side.append(tuple(rb[R_D + 16 * k:R_D + 16 * k + 16] for k in (xi, 2 + xi)))
    for k, (upper, lower) in enumerate(side):
        upper, lower = from_up_y * upper, from_low_y * lower
        for same, plus, rim, group in ((0, 16, 48, 0), (32, 40, 56, 8)):
            n = plus - same
            for row, value in (
                (same + n - 1, upper[group + 5:group + 6]),
                (plus + n - 1, upper[group + 7:group + 8]),
                (same, lower[group + 6:group + 7]),
            ):
                px[k, row:row + 1] = px[k, row:row + 1] + value
            row = rim + 7
            px[k, row:row + 1] = (px[k, row:row + 1] - lower[group + 6:group + 7]) * from_low_y

    sets = (
        (t1, x1, 8, 16, 64, (0, 16, 48), 0),
        (t2, x2, 4, 8, 32, (32, 40, 56), 17),
    )
    for t, x, lz, n, lanes, parts, rows_at in sets:
        count = 2 * lz + 1
        same_up = from_up_y * rb[R_YD + rows_at:R_YD + rows_at + count]
        plus_up = from_up_y * rb[R_YD + 32 + rows_at:R_YD + 32 + rows_at + count]
        low = from_low_y * rb[R_YU + 16 + rows_at:R_YU + 16 + rows_at + count]
        for j in range(count):
            t[j, n - 1:n] = t[j, n - 1:n] + same_up[j:j + 1]
            t[j, 2 * n + 7:2 * n + 8] = t[j, 2 * n + 7:2 * n + 8] + plus_up[j:j + 1]
            t[j, 0:1] = t[j, 0:1] + low[j:j + 1]
            t[j, n + 7:n + 8] = (t[j, n + 7:n + 8] - low[j:j + 1]) * from_low_y

        def column(k):
            same, plus, rim = (px[k, s:s + z] for s, z in zip(parts, (n, n, 8)))
            return jnp.concatenate([same, rim, plus], axis=0)

        above, below = from_up_x * column(1), from_low_x * column(2)
        x[...] = (column(0) - roll(below, lanes // 2)) * from_low_x
        lane = lax.broadcasted_iota(jnp.int32, above.shape, 1)
        at_end = (lane == lanes - 1) | (lane == 2 * lanes - 1)
        for j in range(count):
            value = t[j] + jnp.where(at_end, roll(above, lanes - 1 - j), 0.0)
            t[j] = value + jnp.where(lane == 0, roll(below, -(lanes // 2) - j), 0.0)

    pending = []

    def expand(t, x, v, o, nz, ny, n):
        done = [set() for _ in range(3)]
        rows = {0: slice(ny + 7, 2 * ny + 7), 1: slice(0, ny), 2: slice(ny + 8, 2 * ny + 8)}
        for k in range(2 * nz + 1):
            value = t[k]
            first = 0.0 if x is None else roll(x[...], -(n + k))
            lane = lax.broadcasted_iota(jnp.int32, value.shape, 1)
            low = jnp.where(lane == 0, first, roll(value, 1 - n))
            planes = (low, value, roll(value, -n))
            if k < nz:
                targets = [(1, k)]
            else:
                targets = [(0, k - nz)] if k - nz < nz else []
                targets += [(2, k - nz - 1)] if k > nz else []
            for c, plane in enumerate(planes):
                plane = plane[:, 0:n]
                for a, layer in targets:
                    for b in range(3):
                        v[9 * a + 3 * b + c, layer] = plane[rows[b]]
            for a, layer in targets:
                done[a].add(layer)
                if len(done[a]) == nz:
                    part = pl.ds(9 * a, 9)
                    copy = pltpu.make_async_copy(v.at[part], o.at[part], osem.at[len(pending)])
                    copy.start()
                    pending.append(copy)

    expand(t1, x1, v1, o1, 8, 16, 64)
    expand(t2, x2, v2, o2, 4, 8, 32)

    for c in loads[4:]:
        c.wait()
    blocks = jnp.concatenate(split(g3[...].reshape(384, 128)), axis=1)
    spread = dot(blocks, qx[...])
    lane = lax.broadcasted_iota(jnp.int32, (24, 128), 1)
    for by in range(4):
        for layer in range(3):
            total = None
            for bx in range(4):
                at = 24 * (4 * by + bx)
                part = spread[at:at + 24, 128 * layer:128 * layer + 128]
                if bx != 1:
                    part = roll(part, 16 * (bx - 1))
                if bx == 0:
                    part = jnp.where((lane == 63) | (lane == 127), 0.0, part)
                total = plus_of(total, part)
            q3[24 * by:24 * by + 24, 128 * layer:128 * layer + 128] = total
    for h in range(2):
        rows = jnp.concatenate(
            [q3[24 * by + 8 * h:24 * by + 8 * h + 16, :] for by in range(4)], axis=0
        )
        placed = dot(qy[h], jnp.concatenate(split(rows), axis=0))
        for j in range(3):
            if 3 * h + j < 5:
                s3[3 * h + j] = placed[0:40, 128 * j:128 * j + 128]
    expand(s3, None, v3, o3, 2, 16, 64)
    for copy in pending:
        copy.wait()


def shards(coeff_z, coeff_y, coeff_x, reaction):
    hbm = pl.BlockSpec(memory_space=pltpu.HBM)
    shape = jax.ShapeDtypeStruct
    v = pltpu.VMEM
    dma = pltpu.SemaphoreType.DMA
    pairs = [all_weights(flag, flag) for flag in (False, True)]
    wx, wy = (jnp.asarray(np.stack([pair[k] for pair in pairs])) for k in range(2))
    between = (
        shape((17, 40, 128), F32), shape((9, 24, 128), F32), shape((64, 128), F32),
        shape((R_ROWS, 128), F32), shape((16, 24, 128), F32),
    )
    place = jnp.asarray(np.stack([place_y(4, 4, 48, 16, shift) for shift in (0, 4)]))
    middle = pl.pallas_call(
        main_kernel,
        out_shape=between,
        in_specs=[hbm] * 6,
        out_specs=(hbm,) * 5,
        scratch_shapes=[
            v((4, 16, 32, 128), F32), v((512, 512), BF16), v((64, 512), BF16),
            v((3 * Z_ROWS, 128), F32), v((3 * Z_ROWS, 128), F32),
            v((128, 3 * 128), BF16), v((64, 3 * 128), BF16),
            v((128, 16 * 128), BF16), v((64, 16 * 128), BF16),
            v((128, 11 * 128), BF16), v((64, 11 * 128), BF16),
            v((128, 7 * 128), BF16), v((64, 7 * 128), BF16),
            v((17, 40, 128), F32), v((9, 24, 128), F32), v((5, 16, 128), F32),
            v((S_ROWS, 128), F32), v((24, 128), F32),
            dma((6,)), dma((10,)), dma((10,)), dma((15,)), dma((15,)),
        ],
        compiler_params=pltpu.CompilerParams(
            collective_id=0, has_side_effects=True, vmem_limit_bytes=62 << 20
        ),
    )(reaction, coeff_z, coeff_y, coeff_x, wx, wy)
    return pl.pallas_call(
        finish_kernel,
        out_shape=(
            shape((27, 8, 16, 64), F32), shape((27, 4, 8, 32), F32), shape((27, 2, 16, 64), F32),
        ),
        in_specs=[hbm] * 7,
        out_specs=(hbm,) * 3,
        scratch_shapes=[
            v((17, 40, 128), F32), v((9, 24, 128), F32), v((3, 64, 128), F32),
            v((R_ROWS, 128), F32), v((16, 24, 128), F32),
            v((256, 384), BF16), v((2, 48, 128), BF16), v((40, 128), F32), v((24, 128), F32),
            v((96, 384), F32), v((5, 40, 128), F32),
            v((27, 8, 16, 64), F32), v((27, 4, 8, 32), F32), v((27, 2, 16, 64), F32),
            dma((7,)), dma((9,)),
        ],
        compiler_params=pltpu.CompilerParams(vmem_limit_bytes=62 << 20),
    )(*middle, jnp.asarray(place_x(16)), place)


def solution(mesh):
    in_specs = (P("gz", "gy", "gx"),) * 4
    out_specs = (P(None, "gz", "gy", "gx"), P(None, "gz", "gy", "gx"), P(None, "gz", None, None))
    return jax.shard_map(shards, mesh=mesh, in_specs=in_specs, out_specs=out_specs, check_vma=False)
```

```python
from functools import partial

import jax
import jax.numpy as jnp
import ml_dtypes
import numpy as np
from jax import lax
from jax.experimental import pallas as pl
from jax.experimental.pallas import tpu as pltpu
from jax.sharding import PartitionSpec as P

MESH = pl.DeviceIdType.MESH
F32 = jnp.float32
BF16 = jnp.bfloat16


def forms(level, n, last):
    step = 1 << level
    i = np.arange(n)

    def hat(i, index):
        value = np.maximum(0.0, 1.0 - np.abs(i - (step * index + step - 1)) / step)
        return np.where((i >= n) | (index >= n // step), 0.0, value) if last else value

    def slope(i, index):
        return hat(i, index) - hat(i + 1, index)

    def column(plus, index):
        other = index + plus
        return hat(i, index) * hat(i, other), slope(i, index) * slope(i, other)

    return column


def row_order(count):
    return (
        [(0, j) for j in range(count)]
        + [(1, j) for j in range(-1, count)]
        + [(0, -1), (0, count)]
    )


def y_rows(level, count):
    order = row_order(count)
    if level == 3:
        return dict(zip(order, range(len(order))))
    place = {(0, j): j for j in range(count)}
    place.update({(1, j): count + 8 + j for j in range(count)})
    place.update({(0, -1): count + 5, (0, count): count + 6, (1, -1): count + 7})
    return place


def weights_y(level, n, rows, last):
    column = forms(level, n, last)
    mass = np.zeros((rows, n))
    stiff = np.zeros((rows, n))
    for (plus, index), row in y_rows(level, n >> level).items():
        mass[row], stiff[row] = column(plus, index)
    first = np.concatenate([mass, mass, stiff, stiff], axis=1)
    second = np.concatenate([mass, mass], axis=1)
    return first, second


def lanes_of(level, n):
    count = n >> level
    if level == 3:
        return [(0, j) for j in range(-1, count + 1)] + [(1, j) for j in range(-1, count)], 128
    rim = 2 * count
    lanes = [(0, j) for j in range(count)] + [(1, j) for j in range(count)]
    lanes += [None] * (2 * count)
    lanes[rim] = (0, -1)
    lanes[rim + count // 2] = (0, count)
    lanes[rim + count] = (1, -1)
    return lanes, 4 * count


def weights_x(level, n, last):
    column = forms(level, n, last)
    lanes, width = lanes_of(level, n)
    mass = np.zeros((n, width))
    stiff = np.zeros((n, width))
    for lane, entry in enumerate(lanes):
        if entry is not None:
            mass[:, lane], stiff[:, lane] = column(*entry)
    scale = 0.5**level
    both = np.concatenate([mass, mass, stiff, stiff], axis=0) * scale
    return both


def place_x(count):
    out = np.zeros((2, 128, 3 * 128))
    for layer in range(3):
        for lane, (plus, index) in enumerate(lanes_of(3, count * 8)[0]):
            out[:, 40 * layer + lane, layer * 128 + plus * 64 + count + index] = 1.0
    return out.reshape(256, 384).astype(ml_dtypes.bfloat16)


def place_y(blocks, count, rows, packed, shift):
    whole = blocks * count
    out = np.zeros((rows, 2, blocks, packed))
    for block in range(blocks):
        for row, (plus, index) in enumerate(row_order(count)):
            target = block * count + index
            if 0 <= target < whole:
                out[target + plus * (whole + 8), :, block, row + shift] = 1.0
    return out.reshape(rows, 2 * blocks * packed).astype(ml_dtypes.bfloat16)


def split(value):
    high = value.astype(BF16)
    return high, (value - high.astype(F32)).astype(BF16)


def dot(left, right):
    return jnp.dot(left, right, preferred_element_type=F32)


def roll(value, shift):
    return pltpu.roll(value, shift % 128, 1)


def mass_layers(field):
    n = len(field)
    quarter = [0.25 * field[2 * j] for j in range(n // 2)] + [None]
    same = {-1: quarter[0]}
    plus = {-1: quarter[0]}
    for j in range(n // 2):
        total = field[2 * j + 1] + quarter[j]
        same[j] = total if quarter[j + 1] is None else total + quarter[j + 1]
        plus[j] = quarter[j + 1]
    same[n // 2] = None
    return same, plus


def stiff_layers(field):
    n = len(field)
    share = {-1: 0.25 * field[0], n // 2 - 1: 0.25 * field[n - 1]}
    for j in range(n // 2 - 1):
        share[j] = 0.25 * (field[2 * j + 1] + field[2 * j + 2])
    same = {-1: share[-1], n // 2: share[n // 2 - 1]}
    for j in range(n // 2):
        same[j] = share[j - 1] + share[j]
    return same, share


def plus_of(a, b):
    if a is None:
        return b
    return a if b is None else a + b


def coarser(same, plus, count):
    def scaled(value, factor):
        return None if value is None else factor * value

    new_same, new_plus = {}, {}
    half = count // 2
    for j in range(-1, half + 1):
        total = scaled(plus_of(same.get(2 * j), same.get(2 * j + 2)), 0.25)
        for term in (same.get(2 * j + 1), plus.get(2 * j), plus.get(2 * j + 1)):
            total = plus_of(total, term)
        new_same[j] = total
    for j in range(-1, half):
        total = scaled(plus_of(plus.get(2 * j + 1), plus.get(2 * j + 2)), 0.5)
        new_plus[j] = plus_of(total, scaled(same.get(2 * j + 2), 0.25))
    return new_same, new_plus


def all_weights(last_x, last_y):
    x = np.zeros((512, 512))
    for level, start, width in ((1, 0, 256), (2, 256, 128), (3, 384, 128)):
        x[:, start:start + width] = weights_x(level, 128, last_x)
    y = np.zeros((64, 512))
    for level, row, rows, lane in ((1, 0, 48, 0), (2, 0, 32, 256), (3, 48, 16, 0)):
        first, second = weights_y(level, 32, rows, last_y)
        y[row:row + rows, lane:lane + 128] = first
        y[row:row + rows, lane + 128:lane + 192] = second
    return np.concatenate([x, y], axis=0).astype(ml_dtypes.bfloat16)


S_PX, S_YD, S_YU, S_ROWS = 0, 64, 144, 192
R_X, R_YD, R_YU, R_D, R_ROWS = 0, 128, 208, 256, 320
Z_ONE, Z_TWO, Z_THREE, Z_ROWS = 0, 40, 64, 80


def main_kernel(
    r_hbm, kz_hbm, ky_hbm, kx_hbm, w_hbm,
    t1a, t1b, t2, own, rb, g3,
    f4, wx, wy, rims, rimr, zs, zr,
    gaf, gbf, ga1, gb1, ga2, gb2, ga3, gb3, c3, sb, p3,
    lsem, send, recv, gsend, grecv,
):
    gz, gy, gx = lax.axis_index("gz"), lax.axis_index("gy"), lax.axis_index("gx")
    nz, ny, nx = lax.axis_size("gz"), lax.axis_size("gy"), lax.axis_size("gx")
    zp, zm = lax.rem(gz + 1, nz), lax.rem(gz + nz - 1, nz)
    yp, ym = lax.rem(gy + 1, ny), lax.rem(gy + ny - 1, ny)
    xp, xm = lax.rem(gx + 1, nx), lax.rem(gx + nx - 1, nx)
    slab = ny * nx
    me = gy * nx + gx
    offsets = [(dy, dx) for dx in (2, 1, 3, 0) for dy in (2, 1, 3, 0) if dy or dx]
    peers = [(gz, lax.rem(gy + dy, ny), lax.rem(gx + dx, nx)) for dy, dx in offsets]

    barrier = pltpu.get_barrier_semaphore()
    others = [(zp, gy, gx), (zm, gy, gx)]
    for device in others + peers:
        pl.semaphore_signal(barrier, inc=1, device_id=device, device_id_type=MESH)

    end_x = jnp.where(gx == nx - 1, 1, 0)
    end_y = jnp.where(gy == ny - 1, 1, 0)
    loads = [
        pltpu.make_async_copy(f, f4.at[j], lsem.at[j])
        for j, f in enumerate((r_hbm, kz_hbm, ky_hbm, kx_hbm))
    ]
    loads.append(pltpu.make_async_copy(w_hbm.at[end_x, pl.ds(0, 512)], wx, lsem.at[4]))
    loads.append(pltpu.make_async_copy(w_hbm.at[end_y, pl.ds(512, 64)], wy, lsem.at[5]))
    for c in loads:
        c.start()

    started = []

    def copy(src, dst, device):
        k = len(started)
        c = pltpu.make_async_remote_copy(
            src_ref=src, dst_ref=dst, send_sem=send.at[k], recv_sem=recv.at[k],
            device_id=device, device_id_type=MESH,
        )
        c.start()
        started.append(c)
        return c

    for c in loads:
        c.wait()

    def layers(j):
        return [f4[j, k] for k in range(16)]

    same1, plus1 = mass_layers(layers(0))
    ssame, share = stiff_layers(layers(1))
    for j in range(-1, 9):
        same1[j] = plus_of(same1[j], ssame[j])
    for j in range(-1, 8):
        plus1[j] = -share[j] if plus1[j] is None else plus1[j] - share[j]
    level1 = [(same1, plus1), mass_layers(layers(2)), mass_layers(layers(3))]
    level2 = [coarser(*f, 8) for f in level1]
    level3 = [coarser(*f, 4) for f in level2]
    top_z, low_z = gz == nz - 1, gz == 0
    for level, n, factor in ((level1, 8, 3.0), (level2, 4, 15.0), (level3, 2, 63.0)):
        same, plus = level[0]
        last = jnp.where(top_z, same[n], 0.0)
        same[n - 1] = same[n - 1] + factor * last
        plus[n - 1] = plus[n - 1] + last

    zero = jnp.zeros((32, 128), F32)

    def put(ga, gb, j, values):
        lanes = pl.ds(128 * j, 128)
        for base, (ref, value) in enumerate(zip((ga, ga, gb), values)):
            high, low = split(zero if value is None else value)
            start = 64 * base if base < 2 else 0
            ref[start:start + 32, lanes] = high
            ref[start + 32:start + 64, lanes] = low

    def reduce_yx(level, count, places, ga, gb, wya, wyb, wxl, rows):
        order = row_order(count)
        for j, k in enumerate(places):
            plus, index = order[k]
            put(ga, gb, j, [f[plus][index] for f in level])
        size = len(places)
        left = []
        for value in (dot(wya, ga[:, 0:128 * size]), dot(wyb, gb[:, 0:128 * size])):
            stacked = jnp.concatenate(
                [value[:, 128 * j:128 * j + 128] for j in range(size)], axis=0
            )
            left += split(stacked)
        out = dot(jnp.concatenate(left, axis=1), wxl)
        return {k: out[rows * j:rows * j + rows] for j, k in enumerate(places)}

    def reduce_one(places, ga, gb):
        out = reduce_yx(
            level1, 8, places, ga, gb, wy[0:48, 0:128], wy[0:48, 128:192], wx[:, 0:256], 48
        )
        for k, value in out.items():
            side1[k] = value[0:40, 128:256]
            out1[k] = value[0:40, 0:128]

    out3 = reduce_yx(
        level3, 2, range(7), ga3, gb3, wy[48:64, 0:128], wy[48:64, 128:192], wx[:, 384:512], 16
    )
    out2 = reduce_yx(
        level2, 4, range(11), ga2, gb2, wy[0:32, 256:384], wy[0:32, 384:448], wx[:, 256:384], 32
    )
    out2 = {k: value[0:24] for k, value in out2.items()}
    out1, side1 = {}, {}
    reduce_one((8, 17, 18), gaf, gbf)
    lane1 = lax.broadcasted_iota(jnp.int32, (40, 128), 1)
    low_pair, high_one = (lane1 == 65) | (lane1 == 97), lane1 == 69
    for k, (one, two, three) in enumerate(((17, 9, 5), (8, 4, 2), (18, 10, 6))):
        start = Z_ROWS * k
        zs[start + Z_ONE:start + Z_ONE + 40] = out1[one]
        rest = jnp.concatenate([out2[two], out3[three]], axis=0)
        rest = jnp.where(low_pair, roll(side1[one], 65), rest)
        zs[start + Z_TWO:start + Z_ROWS] = jnp.where(high_one, roll(side1[one], 5), rest)
        rims[16 * k:16 * k + 16] = out3[three]
    for j in range(5):
        c3[j] = out3[j]
    pl.semaphore_wait(barrier, slab - 1 + len(others))
    round_z = [
        copy(rims.at[0:32], rimr.at[0:32], (zm, gy, gx)),
        copy(rims.at[32:48], rimr.at[32:48], (zp, gy, gx)),
    ]
    faces = [
        copy(zs.at[pl.ds(0, 2 * Z_ROWS)], zr.at[pl.ds(0, 2 * Z_ROWS)], (zm, gy, gx)),
        copy(zs.at[pl.ds(2 * Z_ROWS, Z_ROWS)], zr.at[pl.ds(2 * Z_ROWS, Z_ROWS)], (zp, gy, gx)),
    ]
    reduce_one(tuple(range(8)) + tuple(range(9, 17)), ga1, gb1)

    lane2 = lax.broadcasted_iota(jnp.int32, (24, 128), 1)
    totals = [None, None]

    def pack(k, one, side, two):
        if one is not None:
            if k < 9:
                t1a[k] = one
            else:
                t1b[k - 9] = one
            totals[0] = plus_of(totals[0], roll(side, k) if k else side)
            for start, row in ((S_YD, 21), (S_YD + 32, 23), (S_YU + 16, 22)):
                sb[start + k:start + k + 1] = one[row:row + 1]
        if two is not None:
            t2[k] = two
            totals[1] = plus_of(
                totals[1], roll(jnp.where(lane2 >= 64, two, 0.0), 64 + k)
            )
            for start, row in ((S_YD, 13), (S_YD + 32, 15), (S_YU + 16, 14)):
                sb[start + 17 + k:start + 18 + k] = two[row:row + 1]

    blank = jnp.zeros((32, 128), F32)
    for start in (S_YD, S_YD + 32, S_YU + 16):
        sb[start:start + 32] = blank
    for k in range(17):
        if k not in (0, 7, 8, 16):
            pack(k, out1[k], side1[k], None)
    for k in range(9):
        if k not in (0, 3, 4, 8):
            pack(k, None, None, out2[k])

    for c in round_z:
        c.wait_recv()
    low = jnp.where(low_z, 0.0, rimr[32:48])
    fix3 = {
        0: low, 1: jnp.where(top_z, 0.0, rimr[0:16]),
        2: -low, 4: jnp.where(top_z, 0.0, rimr[16:32]),
    }
    packed = [None, None]
    for j in range(5):
        value = c3[j] if j not in fix3 else c3[j] + fix3[j]
        if j == 2:
            value = jnp.where(low_z, 0.0, value)
        packed[j // 3] = plus_of(packed[j // 3], roll(value, 40 * (j % 3)) if j % 3 else value)
    p3[0:16] = packed[0]
    p3[12:24] = packed[1][0:12]
    gather = []
    for d, device in enumerate(peers):
        c = pltpu.make_async_remote_copy(
            src_ref=p3, dst_ref=g3.at[me], send_sem=gsend.at[d], recv_sem=grecv.at[d],
            device_id=device, device_id_type=MESH,
        )
        c.start()
        gather.append(c)
    g3[pl.ds(me, 1)] = p3[...][None]

    for c in faces:
        c.wait_recv()

    def came(k, start, rows):
        value = zr[Z_ROWS * k + start:Z_ROWS * k + start + rows]
        return jnp.where(low_z if k == 2 else top_z, 0.0, value)

    def came_side(k):
        value = came(k, Z_TWO, 40)
        return roll(jnp.where(low_pair, value, 0.0), -65) + roll(jnp.where(high_one, value, 0.0), -5)

    def came_two(k):
        value = came(k, Z_TWO, 24)
        return jnp.where((lane2 == 65) | (lane2 == 97) | (lane2 == 69), 0.0, value)

    def fixed(values, n, part):
        low = part(2)
        return {
            0: values[0] + low,
            n - 1: values[n - 1] + part(0),
            n: jnp.where(low_z, 0.0, values[n] - low),
            2 * n: values[2 * n] + part(1),
        }

    one, side = fixed(out1, 8, lambda k: came(k, Z_ONE, 40)), fixed(side1, 8, came_side)
    for k in one:
        pack(k, one[k], side[k], None)
    for k, value in fixed(out2, 4, came_two).items():
        pack(k, None, None, value)
    total1, total2 = totals
    sb[S_PX:S_PX + 16] = total1[0:16]
    sb[S_PX + 16:S_PX + 32] = total1[24:40]
    sb[S_PX + 32:S_PX + 40] = total2[0:8]
    sb[S_PX + 40:S_PX + 48] = total2[16:24]
    for start in (S_PX + 48, S_YD + 64, S_YU):
        sb[start:start + 8] = total1[16:24]
        sb[start + 8:start + 16] = total2[8:16]
    y_to, x_to = (ym, yp), (xm, xp)
    for yi in range(2):
        for xi in range(2):
            k = 16 * (2 * yi + xi)
            copy(
                sb.at[pl.ds(S_PX + 48, 16)], rb.at[pl.ds(R_D + k, 16)], (gz, y_to[yi], x_to[xi])
            )
    for k in range(2):
        copy(sb.at[pl.ds(S_PX, 64)], rb.at[pl.ds(R_X + 64 * k, 64)], (gz, gy, x_to[k]))
    copy(sb.at[pl.ds(S_YD, 80)], rb.at[pl.ds(R_YD, 80)], (gz, ym, gx))
    copy(sb.at[pl.ds(S_YU, 48)], rb.at[pl.ds(R_YU, 48)], (gz, yp, gx))

    own[...] = sb[S_PX:S_PX + 64]
    for c in started[4:]:
        c.wait_recv()
    for c in gather:
        c.wait()
    for c in started:
        c.wait_send()


def finish_kernel(
    t1a, t1b, t2_in, own, rb, g3, q_hbm, o1, o2, o3,
    t1, t2, px, q, x1, x2, q3, s3, v1, v2, v3, csem, osem,
):
    gy, gx = lax.axis_index("gy"), lax.axis_index("gx")
    ny, nx = lax.axis_size("gy"), lax.axis_size("gx")
    load = pltpu.make_async_copy(q_hbm, q, csem.at[0])
    load.start()
    t1[0:9] = t1a[...]
    t1[9:17] = t1b[...]
    t2[...] = t2_in[...]
    px[0] = own[...]

    def present(flag):
        return jnp.where(flag, 1.0, 0.0).astype(F32)

    from_up_y, from_low_y = present(gy < ny - 1), present(gy > 0)
    from_up_x, from_low_x = present(gx < nx - 1), present(gx > 0)

    for k in range(2):
        px[1 + k] = rb[R_X + 64 * k:R_X + 64 * k + 64]
    side = [(rb[R_YD + 64:R_YD + 80], rb[R_YU:R_YU + 16])]
    for xi in range(2):
        side.append(tuple(rb[R_D + 16 * k:R_D + 16 * k + 16] for k in (xi, 2 + xi)))
    for k, (upper, lower) in enumerate(side):
        upper, lower = from_up_y * upper, from_low_y * lower
        for same, plus, rim, group in ((0, 16, 48, 0), (32, 40, 56, 8)):
            n = plus - same
            for row, value in (
                (same + n - 1, upper[group + 5:group + 6]),
                (plus + n - 1, upper[group + 7:group + 8]),
                (same, lower[group + 6:group + 7]),
            ):
                px[k, row:row + 1] = px[k, row:row + 1] + value
            row = rim + 7
            px[k, row:row + 1] = (px[k, row:row + 1] - lower[group + 6:group + 7]) * from_low_y

    sets = (
        (t1, x1, 8, 16, 64, (0, 16, 48), 0),
        (t2, x2, 4, 8, 32, (32, 40, 56), 17),
    )
    for t, x, lz, n, lanes, parts, rows_at in sets:
        count = 2 * lz + 1
        same_up = from_up_y * rb[R_YD + rows_at:R_YD + rows_at + count]
        plus_up = from_up_y * rb[R_YD + 32 + rows_at:R_YD + 32 + rows_at + count]
        low = from_low_y * rb[R_YU + 16 + rows_at:R_YU + 16 + rows_at + count]
        for j in range(count):
            t[j, n - 1:n] = t[j, n - 1:n] + same_up[j:j + 1]
            t[j, 2 * n + 7:2 * n + 8] = t[j, 2 * n + 7:2 * n + 8] + plus_up[j:j + 1]
            t[j, 0:1] = t[j, 0:1] + low[j:j + 1]
            t[j, n + 7:n + 8] = (t[j, n + 7:n + 8] - low[j:j + 1]) * from_low_y

        def column(k):
            same, plus, rim = (px[k, s:s + z] for s, z in zip(parts, (n, n, 8)))
            return jnp.concatenate([same, rim, plus], axis=0)

        above, below = from_up_x * column(1), from_low_x * column(2)
        x[...] = (column(0) - roll(below, lanes // 2)) * from_low_x
        lane = lax.broadcasted_iota(jnp.int32, above.shape, 1)
        at_end = (lane == lanes - 1) | (lane == 2 * lanes - 1)
        for j in range(count):
            value = t[j] + jnp.where(at_end, roll(above, lanes - 1 - j), 0.0)
            t[j] = value + jnp.where(lane == 0, roll(below, -(lanes // 2) - j), 0.0)

    pending = []

    def expand(t, x, v, o, nz, ny, n):
        done = [set() for _ in range(3)]
        rows = {0: slice(ny + 7, 2 * ny + 7), 1: slice(0, ny), 2: slice(ny + 8, 2 * ny + 8)}
        for k in range(2 * nz + 1):
            value = t[k]
            first = 0.0 if x is None else roll(x[...], -(n + k))
            lane = lax.broadcasted_iota(jnp.int32, value.shape, 1)
            low = jnp.where(lane == 0, first, roll(value, 1 - n))
            planes = (low, value, roll(value, -n))
            if k < nz:
                targets = [(1, k)]
            else:
                targets = [(0, k - nz)] if k - nz < nz else []
                targets += [(2, k - nz - 1)] if k > nz else []
            for c, plane in enumerate(planes):
                plane = plane[:, 0:n]
                for a, layer in targets:
                    for b in range(3):
                        v[9 * a + 3 * b + c, layer] = plane[rows[b]]
            for a, layer in targets:
                done[a].add(layer)
                if len(done[a]) == nz:
                    part = pl.ds(9 * a, 9)
                    copy = pltpu.make_async_copy(v.at[part], o.at[part], osem.at[len(pending)])
                    copy.start()
                    pending.append(copy)

    expand(t1, x1, v1, o1, 8, 16, 64)
    expand(t2, x2, v2, o2, 4, 8, 32)

    load.wait()
    blocks = jnp.concatenate(split(g3[...].reshape(384, 128)), axis=1)
    spread = dot(blocks, q[0:256])
    lane = lax.broadcasted_iota(jnp.int32, (24, 128), 1)
    for by in range(4):
        for layer in range(3):
            total = None
            for bx in range(4):
                at = 24 * (4 * by + bx)
                part = spread[at:at + 24, 128 * layer:128 * layer + 128]
                if bx != 1:
                    part = roll(part, 16 * (bx - 1))
                if bx == 0:
                    part = jnp.where((lane == 63) | (lane == 127), 0.0, part)
                total = plus_of(total, part)
            q3[24 * by:24 * by + 24, 128 * layer:128 * layer + 128] = total
    for h in range(2):
        rows = jnp.concatenate(
            [q3[24 * by + 8 * h:24 * by + 8 * h + 16, :] for by in range(4)], axis=0
        )
        placed = dot(q[256 + 48 * h:304 + 48 * h, 0:128], jnp.concatenate(split(rows), axis=0))
        for j in range(3):
            if 3 * h + j < 5:
                s3[3 * h + j] = placed[0:40, 128 * j:128 * j + 128]
    expand(s3, None, v3, o3, 2, 16, 64)
    for copy in pending:
        copy.wait()


def shards(coeff_z, coeff_y, coeff_x, reaction):
    hbm = pl.BlockSpec(memory_space=pltpu.HBM)
    vmem = pl.BlockSpec(memory_space=pltpu.VMEM)
    shape = jax.ShapeDtypeStruct
    v = pltpu.VMEM
    dma = pltpu.SemaphoreType.DMA
    weights = jnp.asarray(np.stack([all_weights(flag, flag) for flag in (False, True)]))
    between = (
        shape((9, 40, 128), F32), shape((8, 40, 128), F32), shape((9, 24, 128), F32),
        shape((64, 128), F32),
        shape((R_ROWS, 128), F32), shape((16, 24, 128), F32),
    )
    place_rows = np.concatenate([place_y(4, 4, 48, 16, shift) for shift in (0, 4)], axis=0)
    place_rows = np.pad(place_rows.astype(np.float32), ((0, 0), (0, 256)))
    place = jnp.asarray(
        np.concatenate([place_x(16).astype(np.float32), place_rows]).astype(ml_dtypes.bfloat16)
    )
    middle = pl.pallas_call(
        main_kernel,
        out_shape=between,
        in_specs=[hbm] * 5,
        out_specs=(vmem,) * 6,
        scratch_shapes=[
            v((4, 16, 32, 128), F32), v((512, 512), BF16), v((64, 512), BF16),
            v((48, 128), F32), v((48, 128), F32),
            v((3 * Z_ROWS, 128), F32), v((3 * Z_ROWS, 128), F32),
            v((128, 3 * 128), BF16), v((64, 3 * 128), BF16),
            v((128, 16 * 128), BF16), v((64, 16 * 128), BF16),
            v((128, 11 * 128), BF16), v((64, 11 * 128), BF16),
            v((128, 7 * 128), BF16), v((64, 7 * 128), BF16),
            v((5, 16, 128), F32),
            v((S_ROWS, 128), F32), v((24, 128), F32),
            dma((6,)), dma((12,)), dma((12,)), dma((15,)), dma((15,)),
        ],
        compiler_params=pltpu.CompilerParams(
            collective_id=0, has_side_effects=True, vmem_limit_bytes=53 << 20
        ),
    )(reaction, coeff_z, coeff_y, coeff_x, weights)
    return pl.pallas_call(
        finish_kernel,
        out_shape=(
            shape((27, 8, 16, 64), F32), shape((27, 4, 8, 32), F32), shape((27, 2, 16, 64), F32),
        ),
        in_specs=[vmem] * 6 + [hbm],
        out_specs=(hbm,) * 3,
        scratch_shapes=[
            v((17, 40, 128), F32), v((9, 24, 128), F32), v((3, 64, 128), F32),
            v((352, 384), BF16), v((40, 128), F32), v((24, 128), F32),
            v((96, 384), F32), v((5, 40, 128), F32),
            v((27, 8, 16, 64), F32), v((27, 4, 8, 32), F32), v((27, 2, 16, 64), F32),
            dma((1,)), dma((9,)),
        ],
        compiler_params=pltpu.CompilerParams(vmem_limit_bytes=53 << 20),
    )(*middle, place)


def solution(mesh):
    in_specs = (P("gz", "gy", "gx"),) * 4
    out_specs = (P(None, "gz", "gy", "gx"), P(None, "gz", "gy", "gx"), P(None, "gz", None, None))
    return jax.shard_map(shards, mesh=mesh, in_specs=in_specs, out_specs=out_specs, check_vma=False)
```

```python
from functools import partial

import jax
import jax.numpy as jnp
import ml_dtypes
import numpy as np
from jax import lax
from jax.experimental import pallas as pl
from jax.experimental.pallas import tpu as pltpu
from jax.sharding import PartitionSpec as P

MESH = pl.DeviceIdType.MESH
F32 = jnp.float32
BF16 = jnp.bfloat16


def forms(level, n, last):
    step = 1 << level
    i = np.arange(n)

    def hat(i, index):
        value = np.maximum(0.0, 1.0 - np.abs(i - (step * index + step - 1)) / step)
        return np.where((i >= n) | (index >= n // step), 0.0, value) if last else value

    def slope(i, index):
        return hat(i, index) - hat(i + 1, index)

    def column(plus, index):
        other = index + plus
        return hat(i, index) * hat(i, other), slope(i, index) * slope(i, other)

    return column


def row_order(count):
    return (
        [(0, j) for j in range(count)]
        + [(1, j) for j in range(-1, count)]
        + [(0, -1), (0, count)]
    )


def y_rows(level, count):
    order = row_order(count)
    if level == 3:
        return dict(zip(order, range(len(order))))
    place = {(0, j): j for j in range(count)}
    place.update({(1, j): count + 8 + j for j in range(count)})
    place.update({(0, -1): count + 5, (0, count): count + 6, (1, -1): count + 7})
    return place


def weights_y(level, n, rows, last):
    column = forms(level, n, last)
    mass = np.zeros((rows, n))
    stiff = np.zeros((rows, n))
    for (plus, index), row in y_rows(level, n >> level).items():
        mass[row], stiff[row] = column(plus, index)
    first = np.concatenate([mass, mass, stiff, stiff], axis=1)
    second = np.concatenate([mass, mass], axis=1)
    return first, second


def lanes_of(level, n):
    count = n >> level
    if level == 3:
        return [(0, j) for j in range(-1, count + 1)] + [(1, j) for j in range(-1, count)], 128
    rim = 2 * count
    lanes = [(0, j) for j in range(count)] + [(1, j) for j in range(count)]
    lanes += [None] * (2 * count)
    lanes[rim] = (0, -1)
    lanes[rim + count // 2] = (0, count)
    lanes[rim + count] = (1, -1)
    return lanes, 4 * count


def weights_x(level, n, last):
    column = forms(level, n, last)
    lanes, width = lanes_of(level, n)
    mass = np.zeros((n, width))
    stiff = np.zeros((n, width))
    for lane, entry in enumerate(lanes):
        if entry is not None:
            mass[:, lane], stiff[:, lane] = column(*entry)
    scale = 0.5**level
    both = np.concatenate([mass, mass, stiff, stiff], axis=0) * scale
    return both


def place_x(count):
    out = np.zeros((128, 3 * 128))
    for layer in range(3):
        for lane, (plus, index) in enumerate(lanes_of(3, count * 8)[0]):
            out[40 * layer + lane, layer * 128 + plus * 64 + count + index] = 1.0
    return out.astype(ml_dtypes.bfloat16)


def place_y(blocks, count, rows, packed, shift):
    whole = blocks * count
    out = np.zeros((rows, 2, blocks, packed))
    for block in range(blocks):
        for row, (plus, index) in enumerate(row_order(count)):
            target = block * count + index
            if 0 <= target < whole:
                out[target + plus * (whole + 8), :, block, row + shift] = 1.0
    return out.reshape(rows, 2 * blocks * packed).astype(ml_dtypes.bfloat16)


def split(value):
    high = value.astype(BF16)
    return high, (value - high.astype(F32)).astype(BF16)


def dot(left, right):
    return jnp.dot(left, right, preferred_element_type=F32)


def roll(value, shift):
    return pltpu.roll(value, shift % 128, 1)


def mass_layers(field):
    n = len(field)
    quarter = [0.25 * field[2 * j] for j in range(n // 2)] + [None]
    same = {-1: quarter[0]}
    plus = {-1: quarter[0]}
    for j in range(n // 2):
        total = field[2 * j + 1] + quarter[j]
        same[j] = total if quarter[j + 1] is None else total + quarter[j + 1]
        plus[j] = quarter[j + 1]
    same[n // 2] = None
    return same, plus


def stiff_layers(field):
    n = len(field)
    share = {-1: 0.25 * field[0], n // 2 - 1: 0.25 * field[n - 1]}
    for j in range(n // 2 - 1):
        share[j] = 0.25 * (field[2 * j + 1] + field[2 * j + 2])
    same = {-1: share[-1], n // 2: share[n // 2 - 1]}
    for j in range(n // 2):
        same[j] = share[j - 1] + share[j]
    return same, share


def plus_of(a, b):
    if a is None:
        return b
    return a if b is None else a + b


def coarser(same, plus, count):
    def scaled(value, factor):
        return None if value is None else factor * value

    new_same, new_plus = {}, {}
    half = count // 2
    for j in range(-1, half + 1):
        total = scaled(plus_of(same.get(2 * j), same.get(2 * j + 2)), 0.25)
        for term in (same.get(2 * j + 1), plus.get(2 * j), plus.get(2 * j + 1)):
            total = plus_of(total, term)
        new_same[j] = total
    for j in range(-1, half):
        total = scaled(plus_of(plus.get(2 * j + 1), plus.get(2 * j + 2)), 0.5)
        new_plus[j] = plus_of(total, scaled(same.get(2 * j + 2), 0.25))
    return new_same, new_plus


def all_weights(last_x, last_y):
    x = np.zeros((512, 512))
    for level, start, width in ((1, 0, 256), (2, 256, 128), (3, 384, 128)):
        x[:, start:start + width] = weights_x(level, 128, last_x)
    y = np.zeros((64, 512))
    for level, row, rows, lane in ((1, 0, 48, 0), (2, 0, 32, 256), (3, 48, 16, 0)):
        first, second = weights_y(level, 32, rows, last_y)
        y[row:row + rows, lane:lane + 128] = first
        y[row:row + rows, lane + 128:lane + 192] = second
    place = np.zeros((128, 512))
    place[:, 0:384] = place_x(16)
    place[0:96, 384:512] = np.concatenate([place_y(4, 4, 48, 16, shift) for shift in (0, 4)])
    return np.concatenate([x, y, place], axis=0).astype(ml_dtypes.bfloat16)


S_PX, S_YD, S_YU, S_ROWS = 0, 64, 144, 192
R_X, R_YD, R_YU, R_D, R_ROWS = 0, 128, 208, 256, 320
Z_ONE, Z_TWO, Z_THREE, Z_ROWS = 0, 40, 64, 80


def main_kernel(
    r_hbm, kz_hbm, ky_hbm, kx_hbm, w_hbm,
    t1a, t1b, t2, own, rb, g3, q1, q2,
    f4, wx, wy, rims, rimr, zs, zr,
    gaf, gbf, ga1, gb1, ga2, gb2, ga3, gb3, c3, sb, p3,
    lsem, send, recv, gsend, grecv,
):
    gz, gy, gx = lax.axis_index("gz"), lax.axis_index("gy"), lax.axis_index("gx")
    nz, ny, nx = lax.axis_size("gz"), lax.axis_size("gy"), lax.axis_size("gx")
    zp, zm = lax.rem(gz + 1, nz), lax.rem(gz + nz - 1, nz)
    yp, ym = lax.rem(gy + 1, ny), lax.rem(gy + ny - 1, ny)
    xp, xm = lax.rem(gx + 1, nx), lax.rem(gx + nx - 1, nx)
    slab = ny * nx
    me = gy * nx + gx
    offsets = [(dy, dx) for dx in (2, 1, 3, 0) for dy in (2, 1, 3, 0) if dy or dx]
    peers = [(gz, lax.rem(gy + dy, ny), lax.rem(gx + dx, nx)) for dy, dx in offsets]

    barrier = pltpu.get_barrier_semaphore()
    others = [(zp, gy, gx), (zm, gy, gx)]
    for device in others + peers:
        pl.semaphore_signal(barrier, inc=1, device_id=device, device_id_type=MESH)

    end_x = jnp.where(gx == nx - 1, 1, 0)
    end_y = jnp.where(gy == ny - 1, 1, 0)
    loads = [
        pltpu.make_async_copy(f, f4.at[j], lsem.at[j])
        for j, f in enumerate((r_hbm, kz_hbm, ky_hbm, kx_hbm))
    ]
    loads.append(pltpu.make_async_copy(w_hbm.at[end_x, pl.ds(0, 512)], wx, lsem.at[4]))
    loads.append(pltpu.make_async_copy(w_hbm.at[end_y, pl.ds(512, 64)], wy, lsem.at[5]))
    later = [
        pltpu.make_async_copy(w_hbm.at[0, pl.ds(576, 128), pl.ds(0, 384)], q1, lsem.at[6]),
        pltpu.make_async_copy(w_hbm.at[0, pl.ds(576, 96), pl.ds(384, 128)], q2, lsem.at[7]),
    ]
    for c in loads + later:
        c.start()

    started = []

    def copy(src, dst, device):
        k = len(started)
        c = pltpu.make_async_remote_copy(
            src_ref=src, dst_ref=dst, send_sem=send.at[k], recv_sem=recv.at[k],
            device_id=device, device_id_type=MESH,
        )
        c.start()
        started.append(c)
        return c

    for c in loads:
        c.wait()

    def layers(j):
        return [f4[j, k] for k in range(16)]

    same1, plus1 = mass_layers(layers(0))
    ssame, share = stiff_layers(layers(1))
    for j in range(-1, 9):
        same1[j] = plus_of(same1[j], ssame[j])
    for j in range(-1, 8):
        plus1[j] = -share[j] if plus1[j] is None else plus1[j] - share[j]
    level1 = [(same1, plus1), mass_layers(layers(2)), mass_layers(layers(3))]
    level2 = [coarser(*f, 8) for f in level1]
    level3 = [coarser(*f, 4) for f in level2]
    top_z, low_z = gz == nz - 1, gz == 0
    for level, n, factor in ((level1, 8, 3.0), (level2, 4, 15.0), (level3, 2, 63.0)):
        same, plus = level[0]
        last = jnp.where(top_z, same[n], 0.0)
        same[n - 1] = same[n - 1] + factor * last
        plus[n - 1] = plus[n - 1] + last

    zero = jnp.zeros((32, 128), F32)

    def put(ga, gb, j, values):
        lanes = pl.ds(128 * j, 128)
        for base, (ref, value) in enumerate(zip((ga, ga, gb), values)):
            high, low = split(zero if value is None else value)
            start = 64 * base if base < 2 else 0
            ref[start:start + 32, lanes] = high
            ref[start + 32:start + 64, lanes] = low

    def reduce_yx(level, count, places, ga, gb, wya, wyb, wxl, rows):
        order = row_order(count)
        for j, k in enumerate(places):
            plus, index = order[k]
            put(ga, gb, j, [f[plus][index] for f in level])
        size = len(places)
        left = []
        for value in (dot(wya, ga[:, 0:128 * size]), dot(wyb, gb[:, 0:128 * size])):
            stacked = jnp.concatenate(
                [value[:, 128 * j:128 * j + 128] for j in range(size)], axis=0
            )
            left += split(stacked)
        out = dot(jnp.concatenate(left, axis=1), wxl)
        return {k: out[rows * j:rows * j + rows] for j, k in enumerate(places)}

    def reduce_one(places, ga, gb):
        out = reduce_yx(
            level1, 8, places, ga, gb, wy[0:48, 0:128], wy[0:48, 128:192], wx[:, 0:256], 48
        )
        for k, value in out.items():
            side1[k] = value[0:40, 128:256]
            out1[k] = value[0:40, 0:128]

    out3 = reduce_yx(
        level3, 2, range(7), ga3, gb3, wy[48:64, 0:128], wy[48:64, 128:192], wx[:, 384:512], 16
    )
    out2 = reduce_yx(
        level2, 4, range(11), ga2, gb2, wy[0:32, 256:384], wy[0:32, 384:448], wx[:, 256:384], 32
    )
    out2 = {k: value[0:24] for k, value in out2.items()}
    out1, side1 = {}, {}
    reduce_one((8, 17, 18), gaf, gbf)
    lane1 = lax.broadcasted_iota(jnp.int32, (40, 128), 1)
    low_pair, high_one = (lane1 == 65) | (lane1 == 97), lane1 == 69
    for k, (one, two, three) in enumerate(((17, 9, 5), (8, 4, 2), (18, 10, 6))):
        start = Z_ROWS * k
        zs[start + Z_ONE:start + Z_ONE + 40] = out1[one]
        rest = jnp.concatenate([out2[two], out3[three]], axis=0)
        rest = jnp.where(low_pair, roll(side1[one], 65), rest)
        zs[start + Z_TWO:start + Z_ROWS] = jnp.where(high_one, roll(side1[one], 5), rest)
        rims[16 * k:16 * k + 16] = out3[three]
    for j in range(5):
        c3[j] = out3[j]
    pl.semaphore_wait(barrier, slab - 1 + len(others))
    round_z = [
        copy(rims.at[0:32], rimr.at[0:32], (zm, gy, gx)),
        copy(rims.at[32:48], rimr.at[32:48], (zp, gy, gx)),
    ]
    faces = [
        copy(zs.at[pl.ds(0, 2 * Z_ROWS)], zr.at[pl.ds(0, 2 * Z_ROWS)], (zm, gy, gx)),
        copy(zs.at[pl.ds(2 * Z_ROWS, Z_ROWS)], zr.at[pl.ds(2 * Z_ROWS, Z_ROWS)], (zp, gy, gx)),
    ]
    reduce_one(tuple(range(8)) + tuple(range(9, 17)), ga1, gb1)

    lane2 = lax.broadcasted_iota(jnp.int32, (24, 128), 1)
    totals = [None, None]

    def pack(k, one, side, two):
        if one is not None:
            if k < 9:
                t1a[k] = one
            else:
                t1b[k - 9] = one
            totals[0] = plus_of(totals[0], roll(side, k) if k else side)
            for start, row in ((S_YD, 21), (S_YD + 32, 23), (S_YU + 16, 22)):
                sb[start + k:start + k + 1] = one[row:row + 1]
        if two is not None:
            t2[k] = two
            totals[1] = plus_of(
                totals[1], roll(jnp.where(lane2 >= 64, two, 0.0), 64 + k)
            )
            for start, row in ((S_YD, 13), (S_YD + 32, 15), (S_YU + 16, 14)):
                sb[start + 17 + k:start + 18 + k] = two[row:row + 1]

    blank = jnp.zeros((32, 128), F32)
    for start in (S_YD, S_YD + 32, S_YU + 16):
        sb[start:start + 32] = blank
    for k in range(17):
        if k not in (0, 7, 8, 16):
            pack(k, out1[k], side1[k], None)
    for k in range(9):
        if k not in (0, 3, 4, 8):
            pack(k, None, None, out2[k])

    for c in round_z:
        c.wait_recv()
    low = jnp.where(low_z, 0.0, rimr[32:48])
    fix3 = {
        0: low, 1: jnp.where(top_z, 0.0, rimr[0:16]),
        2: -low, 4: jnp.where(top_z, 0.0, rimr[16:32]),
    }
    packed = [None, None]
    for j in range(5):
        value = c3[j] if j not in fix3 else c3[j] + fix3[j]
        if j == 2:
            value = jnp.where(low_z, 0.0, value)
        packed[j // 3] = plus_of(packed[j // 3], roll(value, 40 * (j % 3)) if j % 3 else value)
    p3[0:16] = packed[0]
    p3[12:24] = packed[1][0:12]
    gather = []
    for d, device in enumerate(peers):
        c = pltpu.make_async_remote_copy(
            src_ref=p3, dst_ref=g3.at[me], send_sem=gsend.at[d], recv_sem=grecv.at[d],
            device_id=device, device_id_type=MESH,
        )
        c.start()
        gather.append(c)
    g3[pl.ds(me, 1)] = p3[...][None]

    for c in faces:
        c.wait_recv()

    def came(k, start, rows):
        value = zr[Z_ROWS * k + start:Z_ROWS * k + start + rows]
        return jnp.where(low_z if k == 2 else top_z, 0.0, value)

    def came_side(k):
        value = came(k, Z_TWO, 40)
        return roll(jnp.where(low_pair, value, 0.0), -65) + roll(jnp.where(high_one, value, 0.0), -5)

    def came_two(k):
        value = came(k, Z_TWO, 24)
        return jnp.where((lane2 == 65) | (lane2 == 97) | (lane2 == 69), 0.0, value)

    def fixed(values, n, part):
        low = part(2)
        return {
            0: values[0] + low,
            n - 1: values[n - 1] + part(0),
            n: jnp.where(low_z, 0.0, values[n] - low),
            2 * n: values[2 * n] + part(1),
        }

    one, side = fixed(out1, 8, lambda k: came(k, Z_ONE, 40)), fixed(side1, 8, came_side)
    for k in one:
        pack(k, one[k], side[k], None)
    for k, value in fixed(out2, 4, came_two).items():
        pack(k, None, None, value)
    total1, total2 = totals
    sb[S_PX:S_PX + 16] = total1[0:16]
    sb[S_PX + 16:S_PX + 32] = total1[24:40]
    sb[S_PX + 32:S_PX + 40] = total2[0:8]
    sb[S_PX + 40:S_PX + 48] = total2[16:24]
    for start in (S_PX + 48, S_YD + 64, S_YU):
        sb[start:start + 8] = total1[16:24]
        sb[start + 8:start + 16] = total2[8:16]
    y_to, x_to = (ym, yp), (xm, xp)
    for yi in range(2):
        for xi in range(2):
            k = 16 * (2 * yi + xi)
            copy(
                sb.at[pl.ds(S_PX + 48, 16)], rb.at[pl.ds(R_D + k, 16)], (gz, y_to[yi], x_to[xi])
            )
    for k in range(2):
        copy(sb.at[pl.ds(S_PX, 64)], rb.at[pl.ds(R_X + 64 * k, 64)], (gz, gy, x_to[k]))
    copy(sb.at[pl.ds(S_YD, 80)], rb.at[pl.ds(R_YD, 80)], (gz, ym, gx))
    copy(sb.at[pl.ds(S_YU, 48)], rb.at[pl.ds(R_YU, 48)], (gz, yp, gx))

    own[...] = sb[S_PX:S_PX + 64]
    for c in started[4:]:
        c.wait_recv()
    for c in gather + later:
        c.wait()
    for c in started:
        c.wait_send()


def finish_kernel(
    t1a, t1b, t2_in, own, rb, g3, q1, q2, o1, o2, o3,
    t1, t2, x1, x2, q3, s3, v1, v2, v3, osem,
):
    gy, gx = lax.axis_index("gy"), lax.axis_index("gx")
    ny, nx = lax.axis_size("gy"), lax.axis_size("gx")
    t1[0:9] = t1a[...]
    t1[9:17] = t1b[...]
    t2[...] = t2_in[...]

    def present(flag):
        return jnp.where(flag, 1.0, 0.0).astype(F32)

    from_up_y, from_low_y = present(gy < ny - 1), present(gy > 0)
    from_up_x, from_low_x = present(gx < nx - 1), present(gx > 0)

    row8 = lax.broadcasted_iota(jnp.int32, (8, 128), 0)
    first_row, last_row = row8 == 0, row8 == 7

    def at_row(where, group, value):
        return group + jnp.where(where, value, 0.0)

    def y_fixed(same, rim, plus, same_up, plus_up, low):
        same[-1] = at_row(last_row, same[-1], same_up)
        same[0] = at_row(first_row, same[0], low)
        plus[-1] = at_row(last_row, plus[-1], plus_up)
        rim = jnp.where(last_row, (rim - low) * from_low_y, rim)
        return jnp.concatenate(same + [rim] + plus, axis=0)

    sides = [(own, 0, rb[R_YD + 64:R_YD + 80], rb[R_YU:R_YU + 16])]
    for xi in range(2):
        sides.append((
            rb, R_X + 64 * xi, rb[R_D + 16 * xi:R_D + 16 * xi + 16],
            rb[R_D + 32 + 16 * xi:R_D + 48 + 16 * xi],
        ))
    columns = [[], []]
    for ref, start, upper, lower in sides:
        upper, lower = from_up_y * upper, from_low_y * lower
        for level, (same, plus, rim, size) in enumerate(((0, 16, 48, 16), (32, 40, 56, 8))):
            groups = [
                [ref[start + at + 8 * k:start + at + 8 * k + 8] for k in range(size // 8)]
                for at in (same, plus)
            ]
            up, low = upper[8 * level:8 * level + 8], lower[8 * level:8 * level + 8]
            columns[level].append(y_fixed(
                groups[0], ref[start + rim:start + rim + 8], groups[1],
                up[5:6], up[7:8], low[6:7],
            ))

    sets = (
        (0, t1, x1, 8, 16, 64, 0),
        (1, t2, x2, 4, 8, 32, 17),
    )
    for level, t, x, lz, n, lanes, rows_at in sets:
        count = 2 * lz + 1
        same_up = from_up_y * rb[R_YD + rows_at:R_YD + rows_at + count]
        plus_up = from_up_y * rb[R_YD + 32 + rows_at:R_YD + 32 + rows_at + count]
        low = from_low_y * rb[R_YU + 16 + rows_at:R_YU + 16 + rows_at + count]
        for j in range(count):
            t[j, n - 1:n] = t[j, n - 1:n] + same_up[j:j + 1]
            t[j, 2 * n + 7:2 * n + 8] = t[j, 2 * n + 7:2 * n + 8] + plus_up[j:j + 1]
            t[j, 0:1] = t[j, 0:1] + low[j:j + 1]
            t[j, n + 7:n + 8] = (t[j, n + 7:n + 8] - low[j:j + 1]) * from_low_y

        own_column, above, below = columns[level]
        above, below = from_up_x * above, from_low_x * below
        x[...] = (own_column - roll(below, lanes // 2)) * from_low_x
        lane = lax.broadcasted_iota(jnp.int32, above.shape, 1)
        at_end = (lane == lanes - 1) | (lane == 2 * lanes - 1)
        for j in range(count):
            value = t[j] + jnp.where(at_end, roll(above, lanes - 1 - j), 0.0)
            t[j] = value + jnp.where(lane == 0, roll(below, -(lanes // 2) - j), 0.0)

    pending = []

    def expand(t, x, v, o, nz, ny, n):
        done = [set() for _ in range(3)]
        rows = {0: slice(ny + 7, 2 * ny + 7), 1: slice(0, ny), 2: slice(ny + 8, 2 * ny + 8)}
        for k in range(2 * nz + 1):
            value = t[k]
            first = 0.0 if x is None else roll(x[...], -(n + k))
            lane = lax.broadcasted_iota(jnp.int32, value.shape, 1)
            low = jnp.where(lane == 0, first, roll(value, 1 - n))
            planes = (low, value, roll(value, -n))
            if k < nz:
                targets = [(1, k)]
            else:
                targets = [(0, k - nz)] if k - nz < nz else []
                targets += [(2, k - nz - 1)] if k > nz else []
            for c, plane in enumerate(planes):
                plane = plane[:, 0:n]
                for a, layer in targets:
                    for b in range(3):
                        v[9 * a + 3 * b + c, layer] = plane[rows[b]]
            for a, layer in targets:
                done[a].add(layer)
                if len(done[a]) == nz:
                    part = pl.ds(9 * a, 9)
                    copy = pltpu.make_async_copy(v.at[part], o.at[part], osem.at[len(pending)])
                    copy.start()
                    pending.append(copy)

    expand(t1, x1, v1, o1, 8, 16, 64)
    expand(t2, x2, v2, o2, 4, 8, 32)

    high, low = split(g3[...].reshape(384, 128))
    spread = dot(high, q1[...]) + dot(low, q1[...])
    lane = lax.broadcasted_iota(jnp.int32, (24, 128), 1)
    for by in range(4):
        for layer in range(3):
            total = None
            for bx in range(4):
                at = 24 * (4 * by + bx)
                part = spread[at:at + 24, 128 * layer:128 * layer + 128]
                if bx != 1:
                    part = roll(part, 16 * (bx - 1))
                if bx == 0:
                    part = jnp.where((lane == 63) | (lane == 127), 0.0, part)
                total = plus_of(total, part)
            q3[24 * by:24 * by + 24, 128 * layer:128 * layer + 128] = total
    for h in range(2):
        rows = jnp.concatenate(
            [q3[24 * by + 8 * h:24 * by + 8 * h + 16, :] for by in range(4)], axis=0
        )
        placed = dot(q2[48 * h:48 * h + 48], jnp.concatenate(split(rows), axis=0))
        for j in range(3):
            if 3 * h + j < 5:
                s3[3 * h + j] = placed[0:40, 128 * j:128 * j + 128]
    expand(s3, None, v3, o3, 2, 16, 64)
    for copy in pending:
        copy.wait()


def shards(coeff_z, coeff_y, coeff_x, reaction):
    hbm = pl.BlockSpec(memory_space=pltpu.HBM)
    vmem = pl.BlockSpec(memory_space=pltpu.VMEM)
    shape = jax.ShapeDtypeStruct
    v = pltpu.VMEM
    dma = pltpu.SemaphoreType.DMA
    weights = jnp.asarray(np.stack([all_weights(flag, flag) for flag in (False, True)]))
    between = (
        shape((9, 40, 128), F32), shape((8, 40, 128), F32), shape((9, 24, 128), F32),
        shape((64, 128), F32),
        shape((R_ROWS, 128), F32), shape((16, 24, 128), F32),
        shape((128, 384), BF16), shape((96, 128), BF16),
    )
    middle = pl.pallas_call(
        main_kernel,
        out_shape=between,
        in_specs=[hbm] * 5,
        out_specs=(vmem,) * 8,
        scratch_shapes=[
            v((4, 16, 32, 128), F32), v((512, 512), BF16), v((64, 512), BF16),
            v((48, 128), F32), v((48, 128), F32),
            v((3 * Z_ROWS, 128), F32), v((3 * Z_ROWS, 128), F32),
            v((128, 3 * 128), BF16), v((64, 3 * 128), BF16),
            v((128, 16 * 128), BF16), v((64, 16 * 128), BF16),
            v((128, 11 * 128), BF16), v((64, 11 * 128), BF16),
            v((128, 7 * 128), BF16), v((64, 7 * 128), BF16),
            v((5, 16, 128), F32),
            v((S_ROWS, 128), F32), v((24, 128), F32),
            dma((8,)), dma((12,)), dma((12,)), dma((15,)), dma((15,)),
        ],
        compiler_params=pltpu.CompilerParams(
            collective_id=0, has_side_effects=True, vmem_limit_bytes=(52 << 20) + 921600
        ),
    )(reaction, coeff_z, coeff_y, coeff_x, weights)
    return pl.pallas_call(
        finish_kernel,
        out_shape=(
            shape((27, 8, 16, 64), F32), shape((27, 4, 8, 32), F32), shape((27, 2, 16, 64), F32),
        ),
        in_specs=[vmem] * 8,
        out_specs=(hbm,) * 3,
        scratch_shapes=[
            v((17, 40, 128), F32), v((9, 24, 128), F32),
            v((40, 128), F32), v((24, 128), F32),
            v((96, 384), F32), v((5, 40, 128), F32),
            v((27, 8, 16, 64), F32), v((27, 4, 8, 32), F32), v((27, 2, 16, 64), F32),
            dma((9,)),
        ],
        compiler_params=pltpu.CompilerParams(vmem_limit_bytes=(52 << 20) + 921600),
    )(*middle)


def solution(mesh):
    in_specs = (P("gz", "gy", "gx"),) * 4
    out_specs = (P(None, "gz", "gy", "gx"), P(None, "gz", "gy", "gx"), P(None, "gz", None, None))
    return jax.shard_map(shards, mesh=mesh, in_specs=in_specs, out_specs=out_specs, check_vma=False)
```

```python
from functools import partial

import jax
import jax.numpy as jnp
import ml_dtypes
import numpy as np
from jax import lax
from jax.experimental import pallas as pl
from jax.experimental.pallas import tpu as pltpu
from jax.sharding import PartitionSpec as P

MESH = pl.DeviceIdType.MESH
F32 = jnp.float32
BF16 = jnp.bfloat16


def forms(level, n, last):
    step = 1 << level
    i = np.arange(n)

    def hat(i, index):
        value = np.maximum(0.0, 1.0 - np.abs(i - (step * index + step - 1)) / step)
        return np.where((i >= n) | (index >= n // step), 0.0, value) if last else value

    def slope(i, index):
        return hat(i, index) - hat(i + 1, index)

    def column(plus, index):
        other = index + plus
        return hat(i, index) * hat(i, other), slope(i, index) * slope(i, other)

    return column


def row_order(count):
    return (
        [(0, j) for j in range(count)]
        + [(1, j) for j in range(-1, count)]
        + [(0, -1), (0, count)]
    )


def y_rows(level, count):
    order = row_order(count)
    if level == 3:
        return dict(zip(order, range(len(order))))
    place = {(0, j): j for j in range(count)}
    place.update({(1, j): count + 8 + j for j in range(count)})
    place.update({(0, -1): count + 5, (0, count): count + 6, (1, -1): count + 7})
    return place


def weights_y(level, n, rows, last):
    column = forms(level, n, last)
    mass = np.zeros((rows, n))
    stiff = np.zeros((rows, n))
    for (plus, index), row in y_rows(level, n >> level).items():
        mass[row], stiff[row] = column(plus, index)
    first = np.concatenate([mass, mass, stiff, stiff], axis=1)
    second = np.concatenate([mass, mass], axis=1)
    return first, second


def lanes_of(level, n):
    count = n >> level
    if level == 3:
        return [(0, j) for j in range(-1, count + 1)] + [(1, j) for j in range(-1, count)], 128
    rim = 2 * count
    lanes = [(0, j) for j in range(count)] + [(1, j) for j in range(count)]
    lanes += [None] * (2 * count)
    lanes[rim] = (0, -1)
    lanes[rim + count // 2] = (0, count)
    lanes[rim + count] = (1, -1)
    return lanes, 4 * count


def weights_x(level, n, last):
    column = forms(level, n, last)
    lanes, width = lanes_of(level, n)
    mass = np.zeros((n, width))
    stiff = np.zeros((n, width))
    for lane, entry in enumerate(lanes):
        if entry is not None:
            mass[:, lane], stiff[:, lane] = column(*entry)
    scale = 0.5**level
    both = np.concatenate([mass, mass, stiff, stiff], axis=0) * scale
    return both


def place_x(count):
    out = np.zeros((128, 3 * 128))
    for layer in range(3):
        for lane, (plus, index) in enumerate(lanes_of(3, count * 8)[0]):
            out[40 * layer + lane, layer * 128 + plus * 64 + count + index] = 1.0
    return out.astype(ml_dtypes.bfloat16)


def place_y(blocks, count, rows, packed, shift):
    whole = blocks * count
    out = np.zeros((rows, 2, blocks, packed))
    for block in range(blocks):
        for row, (plus, index) in enumerate(row_order(count)):
            target = block * count + index
            if 0 <= target < whole:
                out[target + plus * (whole + 8), :, block, row + shift] = 1.0
    return out.reshape(rows, 2 * blocks * packed).astype(ml_dtypes.bfloat16)


def split(value):
    high = value.astype(BF16)
    return high, (value - high.astype(F32)).astype(BF16)


def dot(left, right):
    return jnp.dot(left, right, preferred_element_type=F32)


def roll(value, shift):
    return pltpu.roll(value, shift % 128, 1)


def mass_layers(field):
    n = len(field)
    quarter = [0.25 * field[2 * j] for j in range(n // 2)] + [None]
    same = {-1: quarter[0]}
    plus = {-1: quarter[0]}
    for j in range(n // 2):
        total = field[2 * j + 1] + quarter[j]
        same[j] = total if quarter[j + 1] is None else total + quarter[j + 1]
        plus[j] = quarter[j + 1]
    same[n // 2] = None
    return same, plus


def stiff_layers(field):
    n = len(field)
    share = {-1: 0.25 * field[0], n // 2 - 1: 0.25 * field[n - 1]}
    for j in range(n // 2 - 1):
        share[j] = 0.25 * (field[2 * j + 1] + field[2 * j + 2])
    same = {-1: share[-1], n // 2: share[n // 2 - 1]}
    for j in range(n // 2):
        same[j] = share[j - 1] + share[j]
    return same, share


def plus_of(a, b):
    if a is None:
        return b
    return a if b is None else a + b


def coarser(same, plus, count):
    def scaled(value, factor):
        return None if value is None else factor * value

    new_same, new_plus = {}, {}
    half = count // 2
    for j in range(-1, half + 1):
        total = scaled(plus_of(same.get(2 * j), same.get(2 * j + 2)), 0.25)
        for term in (same.get(2 * j + 1), plus.get(2 * j), plus.get(2 * j + 1)):
            total = plus_of(total, term)
        new_same[j] = total
    for j in range(-1, half):
        total = scaled(plus_of(plus.get(2 * j + 1), plus.get(2 * j + 2)), 0.5)
        new_plus[j] = plus_of(total, scaled(same.get(2 * j + 2), 0.25))
    return new_same, new_plus


def all_weights(last_x, last_y):
    x = np.zeros((512, 512))
    for level, start, width in ((1, 0, 256), (2, 256, 128), (3, 384, 128)):
        x[:, start:start + width] = weights_x(level, 128, last_x)
    y = np.zeros((64, 512))
    for level, row, rows, lane in ((1, 0, 48, 0), (2, 0, 32, 256), (3, 48, 16, 0)):
        first, second = weights_y(level, 32, rows, last_y)
        y[row:row + rows, lane:lane + 128] = first
        y[row:row + rows, lane + 128:lane + 192] = second
    place = np.zeros((128, 512))
    place[:, 0:384] = place_x(16)
    place[0:96, 384:512] = np.concatenate([place_y(4, 4, 48, 16, shift) for shift in (0, 4)])
    return np.concatenate([x, y, place], axis=0).astype(ml_dtypes.bfloat16)


S_PX, S_YD, S_YU, S_ROWS = 0, 64, 144, 192
R_X, R_YD, R_YU, R_D, R_ROWS = 0, 128, 208, 256, 320
Z_ONE, Z_TWO, Z_THREE, Z_ROWS = 0, 40, 64, 80


def main_kernel(
    r_hbm, kz_hbm, ky_hbm, kx_hbm, w_hbm,
    t1a, t1b, t2, own, rb, g3, q1, q2,
    f4, wx, wy, rims, rimr, zs, zr,
    gaf, gbf, ga1, gb1, ga2, gb2, ga3, gb3, c3, sb, p3,
    lsem, send, recv, gsend, grecv,
):
    gz, gy, gx = lax.axis_index("gz"), lax.axis_index("gy"), lax.axis_index("gx")
    nz, ny, nx = lax.axis_size("gz"), lax.axis_size("gy"), lax.axis_size("gx")
    zp, zm = lax.rem(gz + 1, nz), lax.rem(gz + nz - 1, nz)
    yp, ym = lax.rem(gy + 1, ny), lax.rem(gy + ny - 1, ny)
    xp, xm = lax.rem(gx + 1, nx), lax.rem(gx + nx - 1, nx)
    slab = ny * nx
    me = gy * nx + gx
    offsets = [(dy, dx) for dx in (2, 1, 3, 0) for dy in (2, 1, 3, 0) if dy or dx]
    peers = [(gz, lax.rem(gy + dy, ny), lax.rem(gx + dx, nx)) for dy, dx in offsets]

    barrier = pltpu.get_barrier_semaphore()
    others = [(zp, gy, gx), (zm, gy, gx)]
    for device in others + peers:
        pl.semaphore_signal(barrier, inc=1, device_id=device, device_id_type=MESH)

    end_x = jnp.where(gx == nx - 1, 1, 0)
    end_y = jnp.where(gy == ny - 1, 1, 0)
    loads = [
        pltpu.make_async_copy(f, f4.at[j], lsem.at[j])
        for j, f in enumerate((r_hbm, kz_hbm, ky_hbm, kx_hbm))
    ]
    loads.append(pltpu.make_async_copy(w_hbm.at[end_x, pl.ds(0, 512)], wx, lsem.at[4]))
    loads.append(pltpu.make_async_copy(w_hbm.at[end_y, pl.ds(512, 64)], wy, lsem.at[5]))
    later = [
        pltpu.make_async_copy(w_hbm.at[0, pl.ds(576, 128), pl.ds(0, 384)], q1, lsem.at[6]),
        pltpu.make_async_copy(w_hbm.at[0, pl.ds(576, 96), pl.ds(384, 128)], q2, lsem.at[7]),
    ]
    for c in loads + later:
        c.start()

    started = []

    def copy(src, dst, device):
        k = len(started)
        c = pltpu.make_async_remote_copy(
            src_ref=src, dst_ref=dst, send_sem=send.at[k], recv_sem=recv.at[k],
            device_id=device, device_id_type=MESH,
        )
        c.start()
        started.append(c)
        return c

    for c in loads:
        c.wait()

    def layers(j):
        return [f4[j, k] for k in range(16)]

    same1, plus1 = mass_layers(layers(0))
    ssame, share = stiff_layers(layers(1))
    for j in range(-1, 9):
        same1[j] = plus_of(same1[j], ssame[j])
    for j in range(-1, 8):
        plus1[j] = -share[j] if plus1[j] is None else plus1[j] - share[j]
    level1 = [(same1, plus1), mass_layers(layers(2)), mass_layers(layers(3))]
    level2 = [coarser(*f, 8) for f in level1]
    level3 = [coarser(*f, 4) for f in level2]
    top_z, low_z = gz == nz - 1, gz == 0
    for level, n, factor in ((level1, 8, 3.0), (level2, 4, 15.0), (level3, 2, 63.0)):
        same, plus = level[0]
        last = jnp.where(top_z, same[n], 0.0)
        same[n - 1] = same[n - 1] + factor * last
        plus[n - 1] = plus[n - 1] + last

    zero = jnp.zeros((32, 128), F32)

    def put(ga, gb, j, values):
        lanes = pl.ds(128 * j, 128)
        for base, (ref, value) in enumerate(zip((ga, ga, gb), values)):
            high, low = split(zero if value is None else value)
            start = 64 * base if base < 2 else 0
            ref[start:start + 32, lanes] = high
            ref[start + 32:start + 64, lanes] = low

    def reduce_yx(level, count, places, ga, gb, wya, wyb, wxl, rows):
        order = row_order(count)
        for j, k in enumerate(places):
            plus, index = order[k]
            put(ga, gb, j, [f[plus][index] for f in level])
        size = len(places)
        left = []
        for value in (dot(wya, ga[:, 0:128 * size]), dot(wyb, gb[:, 0:128 * size])):
            stacked = jnp.concatenate(
                [value[:, 128 * j:128 * j + 128] for j in range(size)], axis=0
            )
            left += split(stacked)
        out = dot(jnp.concatenate(left, axis=1), wxl)
        return {k: out[rows * j:rows * j + rows] for j, k in enumerate(places)}

    def reduce_one(places, ga, gb):
        out = reduce_yx(
            level1, 8, places, ga, gb, wy[0:48, 0:128], wy[0:48, 128:192], wx[:, 0:256], 48
        )
        for k, value in out.items():
            side1[k] = value[0:40, 128:256]
            out1[k] = value[0:40, 0:128]

    out3 = reduce_yx(
        level3, 2, range(7), ga3, gb3, wy[48:64, 0:128], wy[48:64, 128:192], wx[:, 384:512], 16
    )
    out2 = reduce_yx(
        level2, 4, range(11), ga2, gb2, wy[0:32, 256:384], wy[0:32, 384:448], wx[:, 256:384], 32
    )
    out2 = {k: value[0:24] for k, value in out2.items()}
    out1, side1 = {}, {}
    reduce_one((8, 17, 18), gaf, gbf)
    lane1 = lax.broadcasted_iota(jnp.int32, (40, 128), 1)
    low_pair, high_one = (lane1 == 65) | (lane1 == 97), lane1 == 69
    for k, (one, two, three) in enumerate(((17, 9, 5), (8, 4, 2), (18, 10, 6))):
        start = Z_ROWS * k
        zs[start + Z_ONE:start + Z_ONE + 40] = out1[one]
        rest = jnp.concatenate([out2[two], out3[three]], axis=0)
        rest = jnp.where(low_pair, roll(side1[one], 65), rest)
        zs[start + Z_TWO:start + Z_ROWS] = jnp.where(high_one, roll(side1[one], 5), rest)
        rims[16 * k:16 * k + 16] = out3[three]
    for j in range(5):
        c3[j] = out3[j]
    pl.semaphore_wait(barrier, slab - 1 + len(others))
    round_z = [
        copy(rims.at[0:32], rimr.at[0:32], (zm, gy, gx)),
        copy(rims.at[32:48], rimr.at[32:48], (zp, gy, gx)),
    ]
    faces = [
        copy(zs.at[pl.ds(0, 2 * Z_ROWS)], zr.at[pl.ds(0, 2 * Z_ROWS)], (zm, gy, gx)),
        copy(zs.at[pl.ds(2 * Z_ROWS, Z_ROWS)], zr.at[pl.ds(2 * Z_ROWS, Z_ROWS)], (zp, gy, gx)),
    ]
    reduce_one(tuple(range(8)) + tuple(range(9, 17)), ga1, gb1)

    lane2 = lax.broadcasted_iota(jnp.int32, (24, 128), 1)
    totals = [None, None]

    def pack(k, one, side, two):
        if one is not None:
            if k < 9:
                t1a[k] = one
            else:
                t1b[k - 9] = one
            totals[0] = plus_of(totals[0], roll(side, k) if k else side)
            for start, row in ((S_YD, 21), (S_YD + 32, 23), (S_YU + 16, 22)):
                sb[start + k:start + k + 1] = one[row:row + 1]
        if two is not None:
            t2[k] = two
            totals[1] = plus_of(
                totals[1], roll(jnp.where(lane2 >= 64, two, 0.0), 64 + k)
            )
            for start, row in ((S_YD, 13), (S_YD + 32, 15), (S_YU + 16, 14)):
                sb[start + 17 + k:start + 18 + k] = two[row:row + 1]

    blank = jnp.zeros((32, 128), F32)
    for start in (S_YD, S_YD + 32, S_YU + 16):
        sb[start:start + 32] = blank
    for k in range(17):
        if k not in (0, 7, 8, 16):
            pack(k, out1[k], side1[k], None)
    for k in range(9):
        if k not in (0, 3, 4, 8):
            pack(k, None, None, out2[k])

    for c in round_z:
        c.wait_recv()
    low = jnp.where(low_z, 0.0, rimr[32:48])
    fix3 = {
        0: low, 1: jnp.where(top_z, 0.0, rimr[0:16]),
        2: -low, 4: jnp.where(top_z, 0.0, rimr[16:32]),
    }
    packed = [None, None]
    for j in range(5):
        value = c3[j] if j not in fix3 else c3[j] + fix3[j]
        if j == 2:
            value = jnp.where(low_z, 0.0, value)
        packed[j // 3] = plus_of(packed[j // 3], roll(value, 40 * (j % 3)) if j % 3 else value)
    p3[0:16] = packed[0]
    p3[12:24] = packed[1][0:12]
    gather = []
    for d, device in enumerate(peers):
        c = pltpu.make_async_remote_copy(
            src_ref=p3, dst_ref=g3.at[me], send_sem=gsend.at[d], recv_sem=grecv.at[d],
            device_id=device, device_id_type=MESH,
        )
        c.start()
        gather.append(c)
    g3[pl.ds(me, 1)] = p3[...][None]

    for c in faces:
        c.wait_recv()

    def came(k, start, rows):
        value = zr[Z_ROWS * k + start:Z_ROWS * k + start + rows]
        return jnp.where(low_z if k == 2 else top_z, 0.0, value)

    def came_side(k):
        value = came(k, Z_TWO, 40)
        return roll(jnp.where(low_pair, value, 0.0), -65) + roll(jnp.where(high_one, value, 0.0), -5)

    def came_two(k):
        value = came(k, Z_TWO, 24)
        return jnp.where((lane2 == 65) | (lane2 == 97) | (lane2 == 69), 0.0, value)

    def fixed(values, n, part):
        low = part(2)
        return {
            0: values[0] + low,
            n - 1: values[n - 1] + part(0),
            n: jnp.where(low_z, 0.0, values[n] - low),
            2 * n: values[2 * n] + part(1),
        }

    one, side = fixed(out1, 8, lambda k: came(k, Z_ONE, 40)), fixed(side1, 8, came_side)
    for k in one:
        pack(k, one[k], side[k], None)
    for k, value in fixed(out2, 4, came_two).items():
        pack(k, None, None, value)
    total1, total2 = totals
    sb[S_PX:S_PX + 16] = total1[0:16]
    sb[S_PX + 16:S_PX + 32] = total1[24:40]
    sb[S_PX + 32:S_PX + 40] = total2[0:8]
    sb[S_PX + 40:S_PX + 48] = total2[16:24]
    for start in (S_PX + 48, S_YD + 64, S_YU):
        sb[start:start + 8] = total1[16:24]
        sb[start + 8:start + 16] = total2[8:16]
    y_to, x_to = (ym, yp), (xm, xp)
    for yi in range(2):
        for xi in range(2):
            k = 16 * (2 * yi + xi)
            copy(
                sb.at[pl.ds(S_PX + 48, 16)], rb.at[pl.ds(R_D + k, 16)], (gz, y_to[yi], x_to[xi])
            )
    for k in range(2):
        copy(sb.at[pl.ds(S_PX, 64)], rb.at[pl.ds(R_X + 64 * k, 64)], (gz, gy, x_to[k]))
    copy(sb.at[pl.ds(S_YD, 80)], rb.at[pl.ds(R_YD, 80)], (gz, ym, gx))
    copy(sb.at[pl.ds(S_YU, 48)], rb.at[pl.ds(R_YU, 48)], (gz, yp, gx))

    own[...] = sb[S_PX:S_PX + 64]
    for c in started[4:]:
        c.wait_recv()
    for c in gather + later:
        c.wait()
    for c in started:
        c.wait_send()


def finish_kernel(
    t1a, t1b, t2_in, own, rb, g3, q1, q2, o1, o2, o3,
    t1, t2, x1, x2, q3, s3, v1, v2, v3, osem,
):
    gy, gx = lax.axis_index("gy"), lax.axis_index("gx")
    ny, nx = lax.axis_size("gy"), lax.axis_size("gx")
    t1[0:9] = t1a[...]
    t1[9:17] = t1b[...]
    t2[...] = t2_in[...]

    def present(flag):
        return jnp.where(flag, 1.0, 0.0).astype(F32)

    from_up_y, from_low_y = present(gy < ny - 1), present(gy > 0)
    from_up_x, from_low_x = present(gx < nx - 1), present(gx > 0)

    row8 = lax.broadcasted_iota(jnp.int32, (8, 128), 0)
    first_row, last_row = row8 == 0, row8 == 7

    def at_row(where, group, value):
        return group + jnp.where(where, value, 0.0)

    def y_fixed(same, rim, plus, same_up, plus_up, low):
        same[-1] = at_row(last_row, same[-1], same_up)
        same[0] = at_row(first_row, same[0], low)
        plus[-1] = at_row(last_row, plus[-1], plus_up)
        rim = jnp.where(last_row, (rim - low) * from_low_y, rim)
        return jnp.concatenate(same + [rim] + plus, axis=0)

    sides = [(own, 0, rb[R_YD + 64:R_YD + 80], rb[R_YU:R_YU + 16])]
    for xi in range(2):
        sides.append((
            rb, R_X + 64 * xi, rb[R_D + 16 * xi:R_D + 16 * xi + 16],
            rb[R_D + 32 + 16 * xi:R_D + 48 + 16 * xi],
        ))
    columns = [[], []]
    for ref, start, upper, lower in sides:
        upper, lower = from_up_y * upper, from_low_y * lower
        for level, (same, plus, rim, size) in enumerate(((0, 16, 48, 16), (32, 40, 56, 8))):
            groups = [
                [ref[start + at + 8 * k:start + at + 8 * k + 8] for k in range(size // 8)]
                for at in (same, plus)
            ]
            up, low = upper[8 * level:8 * level + 8], lower[8 * level:8 * level + 8]
            columns[level].append(y_fixed(
                groups[0], ref[start + rim:start + rim + 8], groups[1],
                up[5:6], up[7:8], low[6:7],
            ))

    sets = (
        (0, t1, x1, 8, 16, 64, 0),
        (1, t2, x2, 4, 8, 32, 17),
    )
    for level, t, x, lz, n, lanes, rows_at in sets:
        count = 2 * lz + 1
        same_up = from_up_y * rb[R_YD + rows_at:R_YD + rows_at + count]
        plus_up = from_up_y * rb[R_YD + 32 + rows_at:R_YD + 32 + rows_at + count]
        low = from_low_y * rb[R_YU + 16 + rows_at:R_YU + 16 + rows_at + count]
        for j in range(count):
            t[j, n - 1:n] = t[j, n - 1:n] + same_up[j:j + 1]
            t[j, 2 * n + 7:2 * n + 8] = t[j, 2 * n + 7:2 * n + 8] + plus_up[j:j + 1]
            t[j, 0:1] = t[j, 0:1] + low[j:j + 1]
            t[j, n + 7:n + 8] = (t[j, n + 7:n + 8] - low[j:j + 1]) * from_low_y

        own_column, above, below = columns[level]
        above, below = from_up_x * above, from_low_x * below
        x[...] = (own_column - roll(below, lanes // 2)) * from_low_x
        lane = lax.broadcasted_iota(jnp.int32, above.shape, 1)
        at_end = (lane == lanes - 1) | (lane == 2 * lanes - 1)
        for j in range(count):
            value = t[j] + jnp.where(at_end, roll(above, lanes - 1 - j), 0.0)
            t[j] = value + jnp.where(lane == 0, roll(below, -(lanes // 2) - j), 0.0)

    pending = []

    def expand(t, x, v, o, nz, ny, n):
        done, step = [0, 0, 0], min(nz, 4)
        rows = {0: slice(ny + 7, 2 * ny + 7), 1: slice(0, ny), 2: slice(ny + 8, 2 * ny + 8)}
        for k in range(2 * nz + 1):
            value = t[k]
            first = 0.0 if x is None else roll(x[...], -(n + k))
            lane = lax.broadcasted_iota(jnp.int32, value.shape, 1)
            low = jnp.where(lane == 0, first, roll(value, 1 - n))
            planes = (low, value, roll(value, -n))
            if k < nz:
                targets = [(1, k)]
            else:
                targets = [(0, k - nz)] if k - nz < nz else []
                targets += [(2, k - nz - 1)] if k > nz else []
            for c, plane in enumerate(planes):
                plane = plane[:, 0:n]
                for a, layer in targets:
                    for b in range(3):
                        v[9 * a + 3 * b + c, layer] = plane[rows[b]]
            for a, _ in targets:
                done[a] += 1
                if done[a] % step == 0:
                    part, depth = pl.ds(9 * a, 9), pl.ds(done[a] - step, step)
                    copy = pltpu.make_async_copy(
                        v.at[part, depth], o.at[part, depth], osem.at[len(pending)]
                    )
                    copy.start()
                    pending.append(copy)

    expand(t1, x1, v1, o1, 8, 16, 64)
    expand(t2, x2, v2, o2, 4, 8, 32)

    high, low = split(g3[...].reshape(384, 128))
    spread = dot(high, q1[...]) + dot(low, q1[...])
    lane = lax.broadcasted_iota(jnp.int32, (24, 128), 1)
    for by in range(4):
        for layer in range(3):
            total = None
            for bx in range(4):
                at = 24 * (4 * by + bx)
                part = spread[at:at + 24, 128 * layer:128 * layer + 128]
                if bx != 1:
                    part = roll(part, 16 * (bx - 1))
                if bx == 0:
                    part = jnp.where((lane == 63) | (lane == 127), 0.0, part)
                total = plus_of(total, part)
            q3[24 * by:24 * by + 24, 128 * layer:128 * layer + 128] = total
    for h in range(2):
        rows = jnp.concatenate(
            [q3[24 * by + 8 * h:24 * by + 8 * h + 16, :] for by in range(4)], axis=0
        )
        placed = dot(q2[48 * h:48 * h + 48], jnp.concatenate(split(rows), axis=0))
        for j in range(3):
            if 3 * h + j < 5:
                s3[3 * h + j] = placed[0:40, 128 * j:128 * j + 128]
    expand(s3, None, v3, o3, 2, 16, 64)
    for copy in pending:
        copy.wait()


def shards(coeff_z, coeff_y, coeff_x, reaction):
    hbm = pl.BlockSpec(memory_space=pltpu.HBM)
    vmem = pl.BlockSpec(memory_space=pltpu.VMEM)
    shape = jax.ShapeDtypeStruct
    v = pltpu.VMEM
    dma = pltpu.SemaphoreType.DMA
    weights = jnp.asarray(np.stack([all_weights(flag, flag) for flag in (False, True)]))
    between = (
        shape((9, 40, 128), F32), shape((8, 40, 128), F32), shape((9, 24, 128), F32),
        shape((64, 128), F32),
        shape((R_ROWS, 128), F32), shape((16, 24, 128), F32),
        shape((128, 384), BF16), shape((96, 128), BF16),
    )
    middle = pl.pallas_call(
        main_kernel,
        out_shape=between,
        in_specs=[hbm] * 5,
        out_specs=(vmem,) * 8,
        scratch_shapes=[
            v((4, 16, 32, 128), F32), v((512, 512), BF16), v((64, 512), BF16),
            v((48, 128), F32), v((48, 128), F32),
            v((3 * Z_ROWS, 128), F32), v((3 * Z_ROWS, 128), F32),
            v((128, 3 * 128), BF16), v((64, 3 * 128), BF16),
            v((128, 16 * 128), BF16), v((64, 16 * 128), BF16),
            v((128, 11 * 128), BF16), v((64, 11 * 128), BF16),
            v((128, 7 * 128), BF16), v((64, 7 * 128), BF16),
            v((5, 16, 128), F32),
            v((S_ROWS, 128), F32), v((24, 128), F32),
            dma((8,)), dma((12,)), dma((12,)), dma((15,)), dma((15,)),
        ],
        compiler_params=pltpu.CompilerParams(
            collective_id=0, has_side_effects=True, vmem_limit_bytes=(52 << 20) + 921600
        ),
    )(reaction, coeff_z, coeff_y, coeff_x, weights)
    return pl.pallas_call(
        finish_kernel,
        out_shape=(
            shape((27, 8, 16, 64), F32), shape((27, 4, 8, 32), F32), shape((27, 2, 16, 64), F32),
        ),
        in_specs=[vmem] * 8,
        out_specs=(hbm,) * 3,
        scratch_shapes=[
            v((17, 40, 128), F32), v((9, 24, 128), F32),
            v((40, 128), F32), v((24, 128), F32),
            v((96, 384), F32), v((5, 40, 128), F32),
            v((27, 8, 16, 64), F32), v((27, 4, 8, 32), F32), v((27, 2, 16, 64), F32),
            dma((12,)),
        ],
        compiler_params=pltpu.CompilerParams(vmem_limit_bytes=(52 << 20) + 921600),
    )(*middle)


def solution(mesh):
    in_specs = (P("gz", "gy", "gx"),) * 4
    out_specs = (P(None, "gz", "gy", "gx"), P(None, "gz", "gy", "gx"), P(None, "gz", None, None))
    return jax.shard_map(shards, mesh=mesh, in_specs=in_specs, out_specs=out_specs, check_vma=False)
```
